32 devices in a mesh: groups: 2 (over x), chan: 16 (over z, y, core).
Axes of the slice: x: 2, y: 2, z: 4, core: 2. Of those that a mesh axis runs over, the one named last changes fastest.
Arguments:
- voltages: bfloat16 [2048, 128, 128], P(('groups', 'chan')), parts along dimension 0, may hold values from -8 to 8
- antenna_usable_mask: int32 [2048], P('groups'), parts along dimension 0, may hold values 0 or 1
- channel_flags: int32 [256], P(('groups', 'chan')), parts along dimension 0, may hold values 0 or 1
Outputs:
- solution: float32 [3, 2048], P(None, 'groups'), parts along dimension 1
- channel_fit: float32 [2, 256, 1024], P(None, ('groups', 'chan')), parts along dimension 1
The draws below stay inside these ranges and needn't reach their ends.
There are 2 independent parts, one for each index of `groups`. The reference program is written for one: setup_inputs(seed, part) draws one part's arguments, and reference() takes and returns one part's arrays. A program takes and returns all parts, laid end to end along the dimension named above; each array names one. Nothing has to cross between parts.
All inputs are finite; a program needn't handle non-finite values. No bound on the sum of `channel_flags` on one device may be relied on, other than what follows from the above.
Results may differ from the reference program's by a relative error of at most 0.0003.
Values may be sent and summed in bfloat16 or wider, within the bound.
No kernel may reach another device: no remote copies, remote signals or barrier semaphores. Data moves between devices by JAX's collectives and lax.ppermute only.
A program may use at most 128 MiB of HBM per device.

```python
import math
import jax
import jax.numpy as jnp
from jax import lax

INPUTS = 1024
SAMPLES = 64
ITERS = 3
CHANNELS = 128


def draw_voltages(key, part):
    key = jax.random.fold_in(key, 11)
    key_amp, key_phase, key_delay, key_signal, key_noise = jax.random.split(key, 5)
    amplitude = jax.random.uniform(key_amp, (INPUTS, 1, 1), jnp.float32, 0.8, 1.25)
    phases = jax.random.uniform(key_phase, (INPUTS, 1, 1), jnp.float32, -0.6, 0.6)
    delays = jax.random.uniform(key_delay, (INPUTS, 1, 1), jnp.float32, -0.08, 0.08)
    position = (jnp.arange(CHANNELS).astype(jnp.float32) + 0.5) / CHANNELS
    angular_frequency = (2.0 * math.pi * position).reshape(1, CHANNELS, 1)
    shape = (INPUTS, CHANNELS, SAMPLES)
    power = 0.6 + 1.2 * position
    noise_re = 0.5 * jax.random.normal(key_noise, shape, jnp.float32)
    noise_im = 0.5 * jax.random.normal(jax.random.fold_in(key_noise, 1), shape, jnp.float32)
    signal = jax.random.normal(key_signal, (1, CHANNELS, 2 * SAMPLES), jnp.float32)
    signal = signal * jnp.sqrt(power / 2.0).reshape(1, CHANNELS, 1)
    signal_re = signal[..., :SAMPLES]
    signal_im = signal[..., SAMPLES:]
    angles = phases + angular_frequency * delays
    cosine = jnp.cos(angles)
    sine = jnp.sin(angles)
    volt_re = amplitude * (cosine * signal_re - sine * signal_im) + noise_re
    volt_im = amplitude * (sine * signal_re + cosine * signal_im) + noise_im
    joined = jnp.concatenate([volt_re, volt_im], axis=-1)
    return jnp.clip(joined, -8.0, 8.0).astype(jnp.bfloat16)


def with_ends(drawn, key, smallest, largest):
    extent = drawn.shape
    index_at = [jax.random.randint(jax.random.fold_in(key, axis), (), 0, extent[axis]) for axis in range(len(extent))]
    drawn = drawn.at[tuple(index_at)].set(smallest)
    longest = extent.index(max(extent))
    index_at[longest] = (index_at[longest] + 1) % extent[longest]
    return drawn.at[tuple(index_at)].set(largest)


def setup_inputs(seed: int = 0, part: int = 0) -> dict:
    splits = jax.random.split(jax.random.key(seed), 4)
    own_keys = jax.random.split(jax.random.fold_in(splits[3], part), 4)
    voltages = draw_voltages(jax.random.fold_in(jax.random.fold_in(splits[3], part), 71), part)
    antenna_usable_mask = with_ends((jax.random.randint(own_keys[1], (INPUTS,), 0, 16) < 15).astype(jnp.int32), jax.random.fold_in(own_keys[1], 1), 0, 1)
    channel_flags = with_ends((jax.random.randint(own_keys[2], (CHANNELS,), 0, 8) < 7).astype(jnp.int32), jax.random.fold_in(own_keys[2], 1), 0, 1)
    return {"voltages": voltages, "antenna_usable_mask": antenna_usable_mask, "channel_flags": channel_flags}


huber_scale = 0.25
damping = 0.5


def correlate_block(channel_rows):
    half = channel_rows.shape[-1] // 2
    values = channel_rows.astype(jnp.float32)
    swapped = jnp.concatenate([values[..., half:], -values[..., :half]], axis=-1)
    stacked = jnp.concatenate([values, swapped], axis=1)
    product = jnp.einsum("kat,kbt->kab", stacked, values, precision=lax.Precision.HIGHEST)
    return (product * (1.0 / half)).astype(jnp.bfloat16)


def channel_normal_terms(visibility_channel, angular_frequency, gain_parameters, antenna_weight):
    inputs = visibility_channel.shape[1]
    angles = gain_parameters[1] + angular_frequency * gain_parameters[2]
    model_re = gain_parameters[0] * jnp.cos(angles)
    model_im = gain_parameters[0] * jnp.sin(angles)
    vis_re = visibility_channel[:inputs].astype(jnp.float32)
    vis_im = visibility_channel[inputs:].astype(jnp.float32)
    pair_re = model_re[:, None] * model_re[None, :] + model_im[:, None] * model_im[None, :]
    pair_im = model_im[:, None] * model_re[None, :] - model_re[:, None] * model_im[None, :]
    residual_real = vis_re - pair_re
    residual_imaginary = vis_im - pair_im
    positions = jnp.arange(inputs)
    baseline_cross_mask = (positions[:, None] != positions[None, :]).astype(jnp.float32)
    robust_weighting = antenna_weight[:, None] * antenna_weight[None, :] * baseline_cross_mask / (1.0 + (residual_real * residual_real + residual_imaginary * residual_imaginary) / huber_scale)
    prod_re = vis_re * pair_re + vis_im * pair_im
    prod_im = vis_im * pair_re - vis_re * pair_im
    return (jnp.sum(robust_weighting * prod_re, axis=1), jnp.sum(robust_weighting * prod_im, axis=1),
            jnp.sum(robust_weighting * (pair_re * pair_re + pair_im * pair_im), axis=1))


def weighted_sums(prod_re, prod_im, curvature, chan_weight, angular_frequency):
    weight_col = chan_weight[:, None]
    freq_col = angular_frequency[:, None]
    return jnp.stack([jnp.sum(weight_col * prod_re, axis=0), jnp.sum(weight_col * prod_im, axis=0),
                      jnp.sum(weight_col * freq_col * prod_im, axis=0), jnp.sum(weight_col * curvature, axis=0),
                      jnp.sum(weight_col * freq_col * curvature, axis=0),
                      jnp.sum(weight_col * freq_col * freq_col * curvature, axis=0)])


def solve_update(gain_parameters, sums):
    determinant = jnp.maximum(sums[3] * sums[5] - sums[4] * sums[4], 1.0)
    step_phase = (sums[5] * sums[1] - sums[4] * sums[2]) / determinant
    step_delay = (sums[3] * sums[2] - sums[4] * sums[1]) / determinant
    amplitude = gain_parameters[0] * (1.0 + damping * (sums[0] - sums[3]) / jnp.maximum(sums[3], 1.0))
    return jnp.stack([amplitude, gain_parameters[1] + damping * step_phase, gain_parameters[2] + damping * step_delay])


def reference(voltages, antenna_usable_mask, channel_flags):
    per_block = math.gcd(CHANNELS, 8)
    turned = jnp.transpose(voltages, (1, 0, 2)).reshape(CHANNELS // per_block, per_block, INPUTS, 2 * SAMPLES)
    visibilities = lax.map(correlate_block, turned)
    angular_frequency = (2.0 * math.pi) * (jnp.arange(CHANNELS).astype(jnp.float32) + 0.5) / CHANNELS
    chan_weight = channel_flags.astype(jnp.float32)
    antenna_weight = antenna_usable_mask.astype(jnp.float32)
    gain_parameters = jnp.concatenate([jnp.ones((1, INPUTS), jnp.float32), jnp.zeros((2, INPUTS), jnp.float32)], axis=0)
    fitted = jnp.zeros((2, CHANNELS, INPUTS), jnp.float32)
    angular_blocks = angular_frequency.reshape(CHANNELS // per_block, per_block)
    for iteration in range(ITERS):
        def block_terms(solver_entry, gain_parameters=gain_parameters):
            return jax.vmap(lambda visibility_channel, channel_frequency: channel_normal_terms(visibility_channel, channel_frequency, gain_parameters, antenna_weight))(solver_entry[0], solver_entry[1])
        prod_re, prod_im, curvature = lax.map(block_terms, (visibilities, angular_blocks))
        prod_re = prod_re.reshape(CHANNELS, INPUTS)
        prod_im = prod_im.reshape(CHANNELS, INPUTS)
        curvature = curvature.reshape(CHANNELS, INPUTS)
        sums = weighted_sums(prod_re, prod_im, curvature, chan_weight, angular_frequency)
        fitted = jnp.stack([prod_re, prod_im]) / jnp.maximum(curvature, 1.0)[None]
        gain_parameters = solve_update(gain_parameters, sums)
    return gain_parameters, fitted
```

```python
import math

import jax
import jax.numpy as jnp
from jax import lax
from jax.experimental import pallas as pl
from jax.experimental.pallas import tpu as pltpu
from jax.sharding import PartitionSpec as P

ITERS = 3
TILE = 128
VMEM_LIMIT = 48 * 1024 * 1024

huber_scale = 0.25
damping = 0.5


def solve_update(gains, sums):
    determinant = jnp.maximum(sums[3] * sums[5] - sums[4] * sums[4], 1.0)
    step_phase = (sums[5] * sums[1] - sums[4] * sums[2]) / determinant
    step_delay = (sums[3] * sums[2] - sums[4] * sums[1]) / determinant
    amplitude = gains[0] * (1.0 + damping * (sums[0] - sums[3]) / jnp.maximum(sums[3], 1.0))
    return jnp.concatenate(
        [amplitude, gains[1] + damping * step_phase, gains[2] + damping * step_delay], axis=0
    )


def rows_of(ref, count):
    return [ref[k : k + 1, :] for k in range(count)]


def group_rows(tile_row, tiles):
    return 32 if tiles - tile_row > 4 else (64 if tiles - tile_row > 2 else TILE)


def pair_sums(c, tiles, load_vis, row_terms, col_terms, terms, cols_ref, rows_ref):
    cols_ref[...] = jnp.zeros_like(cols_ref)
    for ti in range(tiles):
        group = group_rows(ti, tiles)

        def body(g, carry, ti=ti, group=group):
            first_row = pl.multiple_of(g * group, group)
            row = pl.multiple_of(ti * TILE + first_row, group)
            row_fac = row_terms(row, group)
            totals = None
            for tj in range(ti, tiles):
                vis_re, vis_im = load_vis(ti, tj, first_row, group)
                keep = None
                if tj == ti:
                    ids = lax.broadcasted_iota(jnp.int32, (group, TILE), 0) + first_row
                    keep = ids != lax.broadcasted_iota(jnp.int32, (group, TILE), 1)
                got = terms(vis_re, vis_im, row_fac, col_terms(tj), keep)
                totals = got if totals is None else [a + b for a, b in zip(totals, got)]
                if tj > ti:
                    for k in range(3):
                        part = got[k].reshape(group // 8, 8, TILE).sum(axis=0)
                        at = pl.ds(tj * TILE, TILE)
                        cols_ref[k, :, at] += part if k != 1 else -part
            lanes = lax.broadcasted_iota(jnp.int32, (group, TILE), 1)
            kept = rows_ref[pl.ds(row, group), :]
            for k in range(3):
                kept = jnp.where(lanes == 8 * k + c, jnp.sum(totals[k], axis=1, keepdims=True), kept)
            rows_ref[pl.ds(row, group), :] = kept
            return carry

        lax.fori_loop(0, TILE // group, body, 0)


def store_cols(c, cols_ref, colsum_ref):
    for k in range(3):
        colsum_ref[c, k : k + 1, :] = jnp.sum(cols_ref[k], axis=0, keepdims=True)


def channel_totals(tiles, rows_ref, colsum_ref):
    turned = [rows_ref[t * TILE : (t + 1) * TILE, :].T for t in range(tiles)]
    chans = colsum_ref.shape[0]
    return [
        jnp.concatenate([t[8 * k : 8 * k + chans] for t in turned], axis=1) + colsum_ref[:, k, :]
        for k in range(3)
    ]


def store_sums(totals, weight, freq, sums_ref):
    prod_re, prod_im, curvature = totals
    wim = weight * prod_im
    wcu = weight * curvature
    sums_ref[...] = jnp.concatenate(
        [
            jnp.sum(x, axis=0, keepdims=True)
            for x in (weight * prod_re, wim, freq * wim, wcu, freq * wcu, freq * freq * wcu)
        ],
        axis=0,
    )


def off_diagonal(ti, tj, tiles):
    return sum(tiles - t for t in range(ti)) + tj - ti


def first_kernel(mask_ref, weight_ref, freq_ref, x_ref, vis_ref, sums_ref,
                 wide_ref, chan_ref, swap_ref, maskrow_ref, cols_ref, rows_ref, colsum_ref):
    c = pl.program_id(0)
    inputs, chans, width = x_ref.shape
    tiles = inputs // TILE
    half = width // 2

    @pl.when(c == 0)
    def _():
        rows_ref[...] = jnp.zeros_like(rows_ref)
        for t in range(tiles):
            block = x_ref[t * TILE : (t + 1) * TILE].astype(jnp.float32)
            wide_ref[pl.ds(t * TILE * chans, TILE * chans), :] = block.reshape(TILE * chans, width)
            wide = jnp.broadcast_to(mask_ref[:, t * TILE : (t + 1) * TILE], (TILE, TILE))
            maskrow_ref[t * TILE : (t + 1) * TILE, :] = wide.T

    for t in range(tiles):
        rows = wide_ref[pl.ds(t * TILE * chans + c, TILE, stride=chans), :]
        chan_ref[t * TILE : (t + 1) * TILE, :] = rows.astype(jnp.bfloat16)
        turned = pltpu.roll(rows, half, 1)
        lanes = lax.broadcasted_iota(jnp.int32, rows.shape, 1)
        swap_ref[t * TILE : (t + 1) * TILE, :] = jnp.where(lanes < half, turned, -turned).astype(
            jnp.bfloat16
        )

    for ti in range(tiles):
        right = chan_ref[ti * TILE :, :]
        for part, left_ref in enumerate((chan_ref, swap_ref)):
            left = left_ref[ti * TILE : (ti + 1) * TILE, :]
            product = lax.dot_general(
                left, right, (((1,), (1,)), ((), ())), preferred_element_type=jnp.float32
            )
            scaled = (product * (1.0 / half)).astype(jnp.bfloat16)
            for tj in range(ti, tiles):
                at = (tj - ti) * TILE
                vis_ref[0, off_diagonal(ti, tj, tiles), part] = scaled[:, at : at + TILE]

    def load_vis(ti, tj, first_row, group):
        k = off_diagonal(ti, tj, tiles)
        return [vis_ref[0, k, p, pl.ds(first_row, group), :].astype(jnp.float32) for p in (0, 1)]

    def row_terms(row, group):
        return maskrow_ref[pl.ds(row, group), :]

    def col_terms(tj):
        return mask_ref[:, tj * TILE : (tj + 1) * TILE]

    def terms(vis_re, vis_im, row_mask, col_mask, keep):
        off = vis_re - 1.0
        weight = row_mask * col_mask
        if keep is not None:
            weight = jnp.where(keep, weight, 0.0)
        robust = weight / (1.0 + (off * off + vis_im * vis_im) * (1.0 / huber_scale))
        return [robust * vis_re, robust * vis_im, robust]

    pair_sums(c, tiles, load_vis, row_terms, col_terms, terms, cols_ref, rows_ref)
    store_cols(c, cols_ref, colsum_ref)

    @pl.when(c == pl.num_programs(0) - 1)
    def _():
        totals = channel_totals(tiles, rows_ref, colsum_ref)
        store_sums(totals, weight_ref[...], freq_ref[...], sums_ref)


def next_kernel(gains_ref, old_ref, mask_ref, weight_ref, freq_ref, vis_ref,
                sums_ref, new_ref, fit_ref,
                model_ref, rowfac_ref, cols_ref, rows_ref, colsum_ref):
    c = pl.program_id(0)
    inputs = mask_ref.shape[1]
    tiles = inputs // TILE

    @pl.when(c == 0)
    def _():
        rows_ref[...] = jnp.zeros_like(rows_ref)
        gains = solve_update(rows_of(gains_ref, 3), rows_of(old_ref, 6))
        new_ref[...] = gains
        angles = gains[1:2] + freq_ref[...] * gains[2:3]
        amplitude = gains[0:1] * mask_ref[...]
        model_ref[:, 0, :] = amplitude * jnp.cos(angles)
        model_ref[:, 1, :] = amplitude * jnp.sin(angles)
        model_ref[:, 2, :] = jnp.broadcast_to(amplitude * amplitude, angles.shape)

    for k in range(3):
        for t in range(tiles):
            fac = model_ref[c, k : k + 1, t * TILE : (t + 1) * TILE]
            rowfac_ref[k, t * TILE : (t + 1) * TILE, :] = jnp.broadcast_to(fac, (TILE, TILE)).T

    def load_vis(ti, tj, first_row, group):
        k = off_diagonal(ti, tj, tiles)
        return [vis_ref[0, k, p, pl.ds(first_row, group), :].astype(jnp.float32) for p in (0, 1)]

    def row_terms(row, group):
        return [rowfac_ref[k, pl.ds(row, group), :] for k in range(3)]

    def col_terms(tj):
        return [model_ref[c, k : k + 1, tj * TILE : (tj + 1) * TILE] for k in range(3)]

    def terms(vis_re, vis_im, row_fac, col_fac, keep):
        pair_re = row_fac[0] * col_fac[0] + row_fac[1] * col_fac[1]
        pair_im = row_fac[1] * col_fac[0] - row_fac[0] * col_fac[1]
        off_re = vis_re - pair_re
        off_im = vis_im - pair_im
        robust = 1.0 / (1.0 + (off_re * off_re + off_im * off_im) * (1.0 / huber_scale))
        if keep is not None:
            robust = jnp.where(keep, robust, 0.0)
        return [
            robust * (vis_re * pair_re + vis_im * pair_im),
            robust * (vis_im * pair_re - vis_re * pair_im),
            robust * (row_fac[2] * col_fac[2]),
        ]

    pair_sums(c, tiles, load_vis, row_terms, col_terms, terms, cols_ref, rows_ref)
    store_cols(c, cols_ref, colsum_ref)

    @pl.when(c == pl.num_programs(0) - 1)
    def _():
        totals = channel_totals(tiles, rows_ref, colsum_ref)
        store_sums(totals, weight_ref[...], freq_ref[...], sums_ref)
        bound = jnp.maximum(totals[2], 1.0)
        fit_ref[0] = totals[0] / bound
        fit_ref[1] = totals[1] / bound


def whole(shape):
    return pl.BlockSpec(shape, lambda c: (0,) * len(shape))


def first_iteration(x, mask, weight, freq):
    inputs, chans, width = x.shape
    tiles = inputs // TILE
    blocks = tiles * (tiles + 1) // 2
    return pl.pallas_call(
        first_kernel,
        grid=(chans,),
        in_specs=[whole(mask.shape), whole(weight.shape), whole(freq.shape), whole(x.shape)],
        out_specs=[
            pl.BlockSpec((1, blocks, 2, TILE, TILE), lambda c: (c, 0, 0, 0, 0)),
            whole((6, inputs)),
        ],
        out_shape=[
            jax.ShapeDtypeStruct((chans, blocks, 2, TILE, TILE), jnp.bfloat16),
            jax.ShapeDtypeStruct((6, inputs), jnp.float32),
        ],
        scratch_shapes=[
            pltpu.VMEM((inputs * chans, width), jnp.float32),
            pltpu.VMEM((inputs, width), jnp.bfloat16),
            pltpu.VMEM((inputs, width), jnp.bfloat16),
            pltpu.VMEM((inputs, TILE), jnp.float32),
            pltpu.VMEM((3, 8, inputs), jnp.float32),
            pltpu.VMEM((inputs, TILE), jnp.float32),
            pltpu.VMEM((chans, 8, inputs), jnp.float32),
        ],
        compiler_params=pltpu.CompilerParams(vmem_limit_bytes=VMEM_LIMIT),
        name="first_iteration",
    )(mask, weight, freq, x)


def next_iteration(gains, old_sums, mask, weight, freq, vis):
    chans, blocks = vis.shape[:2]
    inputs = mask.shape[1]
    return pl.pallas_call(
        next_kernel,
        grid=(chans,),
        in_specs=[
            whole(gains.shape), whole(old_sums.shape), whole(mask.shape), whole(weight.shape),
            whole(freq.shape),
            pl.BlockSpec((1, blocks, 2, TILE, TILE), lambda c: (c, 0, 0, 0, 0)),
        ],
        out_specs=[whole((6, inputs)), whole((3, inputs)), whole((2, chans, inputs))],
        out_shape=[
            jax.ShapeDtypeStruct((6, inputs), jnp.float32),
            jax.ShapeDtypeStruct((3, inputs), jnp.float32),
            jax.ShapeDtypeStruct((2, chans, inputs), jnp.float32),
        ],
        scratch_shapes=[
            pltpu.VMEM((chans, 8, inputs), jnp.float32),
            pltpu.VMEM((3, inputs, TILE), jnp.float32),
            pltpu.VMEM((3, 8, inputs), jnp.float32),
            pltpu.VMEM((inputs, TILE), jnp.float32),
            pltpu.VMEM((chans, 8, inputs), jnp.float32),
        ],
        compiler_params=pltpu.CompilerParams(vmem_limit_bytes=VMEM_LIMIT),
        name="next_iteration",
    )(gains, old_sums, mask, weight, freq, vis)


def all_sum(part, devices):
    if devices & (devices - 1):
        return lax.psum(part, "chan")
    reach = 1
    while reach < devices:
        ways = 4 if devices // reach >= 4 else 2
        got = [part] + [
            lax.ppermute(part, "chan", [(i, i ^ (k * reach)) for i in range(devices)])
            for k in range(1, ways)
        ]
        part = (got[0] + got[1]) + (got[2] + got[3]) if ways == 4 else got[0] + got[1]
        reach *= ways
    return part


def local(voltages, antenna_usable_mask, channel_flags):
    devices = lax.axis_size("chan")
    inputs_dev, channels, sample_cols = voltages.shape
    chan_dev = channels // devices
    blocks = voltages.reshape(inputs_dev, devices, chan_dev, sample_cols)
    turned = lax.all_to_all(blocks, "chan", split_axis=1, concat_axis=0, tiled=True)
    inputs = inputs_dev * devices
    arrived = turned.reshape(inputs, chan_dev, sample_cols)
    first_channel = lax.axis_index("chan") * chan_dev
    channel_ids = (first_channel + jnp.arange(chan_dev)).astype(jnp.float32)
    freq = (2.0 * math.pi * (channel_ids + 0.5) / (chan_dev * devices))[:, None]
    weight = channel_flags.astype(jnp.float32)[:, None]
    mask = antenna_usable_mask.astype(jnp.float32)[None, :]
    gains = jnp.concatenate(
        [jnp.ones((1, inputs), jnp.float32), jnp.zeros((2, inputs), jnp.float32)], axis=0
    )
    vis, sums = first_iteration(arrived, mask, weight, freq)
    fitted = None
    for iteration in range(1, ITERS):
        sums, gains, fitted = next_iteration(
            gains, all_sum(sums, devices), mask, weight, freq, vis
        )
    totals = all_sum(sums, devices)
    gains = solve_update([gains[k : k + 1] for k in range(3)], [totals[k : k + 1] for k in range(6)])
    return (gains, fitted)


def solution(mesh):
    placed = (P(("groups", "chan"), None, None), P("groups"), P(("groups", "chan")))
    return jax.shard_map(
        local,
        mesh=mesh,
        in_specs=placed,
        out_specs=(P(None, "groups"), P(None, ("groups", "chan"), None)),
        check_vma=False,
    )
```

```python
import math

import jax
import jax.numpy as jnp
from jax import lax
from jax.experimental import pallas as pl
from jax.experimental.pallas import tpu as pltpu
from jax.sharding import PartitionSpec as P

ITERS = 3
TILE = 128
GROUP = 16
UNIT = 16
PARTS = 2
AHEAD = 1
HUGE = 1e38
VMEM_LIMIT = 20 * 1024 * 1024

huber_scale = 0.25
damping = 0.5


def solve_update(gains, sums):
    determinant = jnp.maximum(sums[3] * sums[5] - sums[4] * sums[4], 1.0)
    step_phase = (sums[5] * sums[1] - sums[4] * sums[2]) / determinant
    step_delay = (sums[3] * sums[2] - sums[4] * sums[1]) / determinant
    amplitude = gains[0] * (1.0 + damping * (sums[0] - sums[3]) / jnp.maximum(sums[3], 1.0))
    return jnp.concatenate(
        [amplitude, gains[1] + damping * step_phase, gains[2] + damping * step_delay], axis=0
    )


def rows_of(ref, count):
    return [ref[k : k + 1, :] for k in range(count)]


def places(tiles):
    out = {}
    for part, rows in enumerate(tile_parts(tiles)):
        pairs = [(ti, tj) for ti in rows for tj in range(ti, tiles)]
        out.update({pair: (part, k) for k, pair in enumerate(pairs)})
    return out


def part_size(tiles):
    return max(k for _, k in places(tiles).values()) + 1


def drain(jobs):
    for _ in jobs:
        pass


def pair_sums(c, rows, tiles, terms, ahead, cols_ref, acc_ref, rows_ref):
    for ti in rows:
        for first in range(0, TILE, GROUP):
            for _ in range(AHEAD):
                next(ahead, None)
            row = ti * TILE + first
            totals = [None] * (GROUP // UNIT)
            for tj in range(ti, tiles):
                parts = None
                for unit in range(GROUP // UNIT):
                    at = first + unit * UNIT
                    keep = None
                    if tj == ti:
                        ids = lax.broadcasted_iota(jnp.int32, (UNIT, TILE), 0) + at
                        keep = ids != lax.broadcasted_iota(jnp.int32, (UNIT, TILE), 1)
                    got = terms(ti, tj, at, keep)
                    if totals[unit] is None:
                        totals[unit] = got
                    else:
                        totals[unit] = [a + b for a, b in zip(totals[unit], got)]
                    if tj > ti:
                        part = [x.reshape(UNIT // 8, 8, TILE).sum(axis=0) for x in got]
                        parts = part if parts is None else [a + b for a, b in zip(parts, part)]
                if tj > ti:
                    lanes = slice(tj * TILE, (tj + 1) * TILE)
                    for k in range(3):
                        cols_ref[k, :, lanes] += parts[k] if k != 1 else -parts[k]
            fold_rows(c - 1, row, GROUP, acc_ref, rows_ref)
            for unit in range(GROUP // UNIT):
                for k in range(3):
                    acc_ref[k, row + unit * UNIT : row + (unit + 1) * UNIT, :] = totals[unit][k]
    drain(ahead)


def tile_parts(tiles):
    order = [r for p in range((tiles + 1) // 2) for r in sorted({p, tiles - 1 - p})]
    size = -(-len(order) // PARTS)
    return [order[k : k + size] for k in range(0, len(order), size)]


def fold_rows(c, row, count, acc_ref, rows_ref):
    lanes = lax.broadcasted_iota(jnp.int32, (count, TILE), 1)
    kept = rows_ref[row : row + count, :]
    for k in range(3):
        total = jnp.sum(acc_ref[k, row : row + count, :], axis=1, keepdims=True)
        kept = jnp.where(lanes == 8 * k + c, total, kept)
    rows_ref[row : row + count, :] = kept


def store_cols(c, cols_ref, colsum_ref):
    for k in range(3):
        colsum_ref[c, k : k + 1, :] = jnp.sum(cols_ref[k], axis=0, keepdims=True)


def channel_totals(tiles, rows_ref, colsum_ref, scales):
    turned = [rows_ref[t * TILE : (t + 1) * TILE, :].T for t in range(tiles)]
    chans = colsum_ref.shape[0]
    return [
        scales[k]
        * (jnp.concatenate([t[8 * k : 8 * k + chans] for t in turned], axis=1) + colsum_ref[:, k, :])
        for k in range(3)
    ]


def store_sums(totals, weight, freq, sums_ref):
    prod_re, prod_im, curvature = totals
    wim = weight * prod_im
    wcu = weight * curvature
    sums_ref[...] = jnp.concatenate(
        [
            jnp.sum(x, axis=0, keepdims=True)
            for x in (weight * prod_re, wim, freq * wim, wcu, freq * wcu, freq * freq * wcu)
        ],
        axis=0,
    )


def first_kernel(mask_ref, weight_ref, freq_ref, x_ref, vis_ref, size_ref, sums_ref,
                 wide_ref, right_ref, left_ref, maskrow_ref, base_ref, cols_ref, acc_ref,
                 rows_ref, colsum_ref):
    c = pl.program_id(0)
    inputs, chans, width = x_ref.shape
    tiles = inputs // TILE
    half = width // 2
    parts, place = tile_parts(tiles), places(tiles)
    last = chans - 1

    def load_channel(c):
        lanes = lax.broadcasted_iota(jnp.int32, (TILE, width), 1)
        slot = lax.rem(c, 2)
        for t in range(tiles):
            at = slice(t * TILE, (t + 1) * TILE)
            rows = wide_ref[pl.ds(t * TILE * chans + c, TILE, stride=chans), :]
            rows = rows * maskrow_ref[at, :]
            right_ref[slot, at, :] = rows.astype(jnp.bfloat16)
            rows = rows + rows
            turned = pltpu.roll(rows, half, 1)
            left_ref[slot, t, :TILE, :] = rows.astype(jnp.bfloat16)
            left_ref[slot, t, TILE:, :] = jnp.where(lanes < half, turned, -turned).astype(jnp.bfloat16)

    def correlate(c, part):
        slot = lax.rem(c, 2)
        for ti in parts[part]:
            yield
            twice = lax.dot_general(
                left_ref[slot, ti], right_ref[slot, ti * TILE :, :], (((1,), (1,)), ((), ())),
                preferred_element_type=jnp.float32,
            ).astype(jnp.bfloat16)
            for tj in range(ti, tiles):
                at = slice((tj - ti) * TILE, (tj - ti + 1) * TILE)
                for p in (0, 1):
                    vis_ref[(c,) + place[ti, tj] + (p,)] = twice[p * TILE : (p + 1) * TILE, at]

    @pl.when(c == 0)
    def _():
        rows_ref[...] = jnp.zeros_like(rows_ref)
        acc_ref[...] = jnp.zeros_like(acc_ref)
        for t in range(tiles):
            at = slice(t * TILE, (t + 1) * TILE)
            block = x_ref[at].astype(jnp.float32)
            wide_ref[pl.ds(t * TILE * chans, TILE * chans), :] = block.reshape(TILE * chans, width)
            maskrow_ref[at, :] = jnp.broadcast_to(mask_ref[:, at] * 0.125, (TILE, TILE)).T
        flagged = (1.0 - mask_ref[...]) * HUGE
        ones = jnp.ones_like(flagged)
        sub = lax.broadcasted_iota(jnp.int32, (16, inputs), 0)
        near = jnp.where(sub == 0, 5.0 * ones, jnp.where(sub == 1, flagged, jnp.where(sub == 2, ones, 0.0)))
        far = jnp.where(sub < 2, ones, jnp.where(sub == 2, flagged, 0.0))
        near, far = near.astype(jnp.bfloat16), far.astype(jnp.bfloat16)
        for ti in range(tiles):
            base = lax.dot_general(
                near[:, ti * TILE : (ti + 1) * TILE], far[:, ti * TILE :], (((0,), (0,)), ((), ())),
                preferred_element_type=jnp.float32,
            )
            for tj in range(ti, tiles):
                base_ref[place[ti, tj]] = base[:, (tj - ti) * TILE : (tj - ti + 1) * TILE]

    @pl.when(c == 0)
    def _():
        load_channel(c)

    @pl.when(c == 0)
    def _():
        drain(correlate(c, 0))

    def terms(ti, tj, first, keep):
        rows = slice(first, first + UNIT)
        part, k = place[ti, tj]
        vis = []
        for p in (0, 1):
            vis.append(vis_ref[c, part, k, p, rows, :].astype(jnp.float32))
        size = vis[0] * vis[0] + vis[1] * vis[1]
        size_ref[c, part, k, rows, :] = size + 1.0
        robust = 1.0 / (size + (base_ref[part, k, rows, :] - 4.0 * vis[0]))
        if keep is not None:
            robust = jnp.where(keep, robust, 0.0)
        return [robust * vis[0], robust * vis[1], robust]

    for part in range(len(parts)):
        @pl.when(c >= -part)
        def _(part=part):
            if part == 0:
                cols_ref[...] = jnp.zeros_like(cols_ref)
            if part + 1 < len(parts):
                ahead = correlate(c, part + 1)
            else:
                ahead = correlate(jnp.minimum(c + 1, last), 0)
            if part == 0:
                load_channel(jnp.minimum(c + 1, last))
            pair_sums(c, parts[part], tiles, terms, ahead, cols_ref, acc_ref, rows_ref)
            if part + 1 == len(parts):
                store_cols(c, cols_ref, colsum_ref)

    @pl.when(c == last)
    def _():
        fold_rows(c, 0, inputs, acc_ref, rows_ref)
        totals = channel_totals(tiles, rows_ref, colsum_ref, (0.5, 0.5, 1.0))
        store_sums(totals, weight_ref[...], freq_ref[...], sums_ref)


def pieces(value):
    out = []
    for _ in range(3):
        out.append(value.astype(jnp.bfloat16).astype(jnp.float32))
        value = value - out[-1]
    return out


def next_kernel(gains_ref, old_ref, mask_ref, weight_ref, freq_ref, vis_ref, size_ref,
                sums_ref, new_ref, fit_ref,
                model_ref, pair_ref, square_ref, left_ref, right_ref, cols_ref, acc_ref, rows_ref,
                colsum_ref):
    c = pl.program_id(0)
    last = pl.num_programs(0) - 1
    inputs = mask_ref.shape[1]
    tiles = inputs // TILE
    parts, place = tile_parts(tiles), places(tiles)
    sub = lax.broadcasted_iota(jnp.int32, (8, inputs), 0)
    zero = jnp.zeros((8, inputs), jnp.float32)

    def spread(piece, count):
        return jnp.broadcast_to(piece, (count, inputs))

    def load_channel(c):
        slot = lax.rem(c, 2)
        for p in (0, 1):
            own = model_ref[c, 8 * p : 8 * p + 8, :]
            left_ref[slot, p] = jnp.concatenate([own] * 3 + [zero], axis=0).astype(jnp.bfloat16)
        right = [
            jnp.where(sub < 3, spread(model_ref[c, k : k + 1, :], 8), spread(model_ref[c, 3 + k : 4 + k, :], 8))
            for k in range(3)
        ]
        right_ref[slot] = jnp.concatenate(right + [zero], axis=0).astype(jnp.bfloat16)

    def model(c, part):
        slot = lax.rem(c, 2)
        for ti in parts[part]:
            for p in (0, 1):
                yield
                pair = lax.dot_general(
                    left_ref[slot, p, :, ti * TILE : (ti + 1) * TILE],
                    right_ref[slot, :, ti * TILE :],
                    (((0,), (0,)), ((), ())),
                    preferred_element_type=jnp.float32,
                )
                for tj in range(ti, tiles):
                    at = slice((tj - ti) * TILE, (tj - ti + 1) * TILE)
                    pair_ref[place[ti, tj] + (p,)] = pair[:, at]

    @pl.when(c == 0)
    def _():
        rows_ref[...] = jnp.zeros_like(rows_ref)
        acc_ref[...] = jnp.zeros_like(acc_ref)
        gains = solve_update(rows_of(gains_ref, 3), rows_of(old_ref, 6))
        new_ref[...] = gains
        angles = gains[1:2] + freq_ref[...] * gains[2:3]
        amplitude = gains[0:1] * mask_ref[...]
        double = amplitude + amplitude
        model_re = pieces(double * jnp.cos(angles))
        model_im = pieces(double * jnp.sin(angles))
        for k in range(3):
            model_ref[:, k, :] = model_re[k]
            model_ref[:, 3 + k, :] = model_im[k]
            model_ref[:, 8 + k, :] = model_im[k]
            model_ref[:, 11 + k, :] = -model_re[k]
        for k in (6, 7, 14, 15):
            model_ref[:, k, :] = jnp.zeros_like(angles)
        b = pieces(double * amplitude)
        b = [jnp.broadcast_to(x, (8, inputs)) for x in b]
        left = jnp.where(sub < 3, b[0], jnp.where(sub < 5, b[1], jnp.where(sub < 6, b[2], 0.0)))
        right = jnp.where(
            (sub == 0) | (sub == 3) | (sub == 5), b[0], jnp.where((sub == 1) | (sub == 4), b[1], b[2])
        )
        left = jnp.concatenate([left, zero], axis=0).astype(jnp.bfloat16)
        right = jnp.concatenate([right, zero], axis=0).astype(jnp.bfloat16)
        for ti in range(tiles):
            square = lax.dot_general(
                left[:, ti * TILE : (ti + 1) * TILE], right[:, ti * TILE :], (((0,), (0,)), ((), ())),
                preferred_element_type=jnp.float32,
            )
            for tj in range(ti, tiles):
                square_ref[place[ti, tj]] = square[:, (tj - ti) * TILE : (tj - ti + 1) * TILE]

    @pl.when(c == 0)
    def _():
        load_channel(c)
        drain(model(c, 0))

    def terms(ti, tj, first, keep):
        part, k = place[ti, tj]
        rows = slice(first, first + UNIT)
        vis_re, vis_im = [vis_ref[c, part, k, p, rows, :].astype(jnp.float32) for p in (0, 1)]
        pair_re, pair_im = [pair_ref[part, k, p, rows, :] for p in (0, 1)]
        square = square_ref[part, k, rows, :]
        prod_re = vis_re * pair_re + vis_im * pair_im
        prod_im = vis_im * pair_re - vis_re * pair_im
        robust = 1.0 / (size_ref[c, part, k, rows, :] - prod_re + square)
        if keep is not None:
            robust = jnp.where(keep, robust, 0.0)
        return [robust * prod_re, robust * prod_im, robust * square]

    for part in range(len(parts)):
        @pl.when(c >= -part)
        def _(part=part):
            if part == 0:
                cols_ref[...] = jnp.zeros_like(cols_ref)
            if part + 1 < len(parts):
                ahead = model(c, part + 1)
            else:
                ahead = model(jnp.minimum(c + 1, last), 0)
            if part == 0:
                load_channel(jnp.minimum(c + 1, last))
            pair_sums(c, parts[part], tiles, terms, ahead, cols_ref, acc_ref, rows_ref)
            if part + 1 == len(parts):
                store_cols(c, cols_ref, colsum_ref)

    @pl.when(c == last)
    def _():
        fold_rows(c, 0, inputs, acc_ref, rows_ref)
        totals = channel_totals(tiles, rows_ref, colsum_ref, (0.125, 0.125, 0.25))
        store_sums(totals, weight_ref[...], freq_ref[...], sums_ref)
        bound = jnp.maximum(totals[2], 1.0)
        fit_ref[0] = totals[0] / bound
        fit_ref[1] = totals[1] / bound


def whole(shape):
    return pl.BlockSpec(shape, lambda c: (0,) * len(shape))


RESIDENT = pl.BlockSpec(memory_space=pltpu.VMEM)


def first_iteration(x, mask, weight, freq):
    inputs, chans, width = x.shape
    tiles = inputs // TILE
    steps, size = len(tile_parts(tiles)), part_size(tiles)
    return pl.pallas_call(
        first_kernel,
        grid=(chans,),
        in_specs=[whole(mask.shape), whole(weight.shape), whole(freq.shape), whole(x.shape)],
        out_specs=[RESIDENT, RESIDENT, whole((6, inputs))],
        out_shape=[
            pltpu.VMEM((chans, steps, size, 2, TILE, TILE), jnp.bfloat16),
            pltpu.VMEM((chans, steps, size, TILE, TILE), jnp.float32),
            jax.ShapeDtypeStruct((6, inputs), jnp.float32),
        ],
        scratch_shapes=[
            pltpu.VMEM((inputs * chans, width), jnp.float32),
            pltpu.VMEM((2, inputs, width), jnp.bfloat16),
            pltpu.VMEM((2, tiles, 2 * TILE, width), jnp.bfloat16),
            pltpu.VMEM((inputs, TILE), jnp.float32),
            pltpu.VMEM((steps, size, TILE, TILE), jnp.float32),
            pltpu.VMEM((3, 8, inputs), jnp.float32),
            pltpu.VMEM((3, inputs, TILE), jnp.float32),
            pltpu.VMEM((inputs, TILE), jnp.float32),
            pltpu.VMEM((chans, 8, inputs), jnp.float32),
        ],
        compiler_params=pltpu.CompilerParams(vmem_limit_bytes=VMEM_LIMIT),
        name="first_iteration",
    )(mask, weight, freq, x)


def held(x):
    return pltpu.with_memory_space_constraint(x, pltpu.VMEM)


def next_iteration(gains, old_sums, mask, weight, freq, vis, size):
    chans, steps, count = size.shape[:3]
    inputs = mask.shape[1]
    tiles = inputs // TILE
    return pl.pallas_call(
        next_kernel,
        grid=(chans,),
        in_specs=[
            whole(gains.shape), whole(old_sums.shape), whole(mask.shape), whole(weight.shape),
            whole(freq.shape),
        ] + [RESIDENT, RESIDENT],
        out_specs=[whole((6, inputs)), whole((3, inputs)), whole((2, chans, inputs))],
        out_shape=[
            jax.ShapeDtypeStruct((6, inputs), jnp.float32),
            jax.ShapeDtypeStruct((3, inputs), jnp.float32),
            jax.ShapeDtypeStruct((2, chans, inputs), jnp.float32),
        ],
        scratch_shapes=[
            pltpu.VMEM((chans, 16, inputs), jnp.float32),
            pltpu.VMEM((steps, count, 2, TILE, TILE), jnp.float32),
            pltpu.VMEM((steps, count, TILE, TILE), jnp.float32),
            pltpu.VMEM((2, 2, 32, inputs), jnp.bfloat16),
            pltpu.VMEM((2, 32, inputs), jnp.bfloat16),
            pltpu.VMEM((3, 8, inputs), jnp.float32),
            pltpu.VMEM((3, inputs, TILE), jnp.float32),
            pltpu.VMEM((inputs, TILE), jnp.float32),
            pltpu.VMEM((chans, 8, inputs), jnp.float32),
        ],
        compiler_params=pltpu.CompilerParams(vmem_limit_bytes=VMEM_LIMIT),
        name="next_iteration",
    )(gains, old_sums, mask, weight, freq, held(vis), held(size))


def all_sum(part, devices):
    if devices & (devices - 1):
        return lax.psum(part, "chan")
    reach = 1
    while reach < devices:
        ways = 4 if devices // reach >= 4 else 2
        got = [part] + [
            lax.ppermute(part, "chan", [(i, i ^ (k * reach)) for i in range(devices)])
            for k in range(1, ways)
        ]
        part = (got[0] + got[1]) + (got[2] + got[3]) if ways == 4 else got[0] + got[1]
        reach *= ways
    return part


def local(voltages, antenna_usable_mask, channel_flags):
    devices = lax.axis_size("chan")
    inputs_dev, channels, sample_cols = voltages.shape
    chan_dev = channels // devices
    blocks = voltages.reshape(inputs_dev, devices, chan_dev, sample_cols)
    turned = lax.all_to_all(blocks, "chan", split_axis=1, concat_axis=0, tiled=True)
    inputs = inputs_dev * devices
    arrived = turned.reshape(inputs, chan_dev, sample_cols)
    first_channel = lax.axis_index("chan") * chan_dev
    channel_ids = (first_channel + jnp.arange(chan_dev)).astype(jnp.float32)
    freq = (2.0 * math.pi * (channel_ids + 0.5) / (chan_dev * devices))[:, None]
    weight = channel_flags.astype(jnp.float32)[:, None]
    mask = antenna_usable_mask.astype(jnp.float32)[None, :]
    gains = jnp.concatenate(
        [jnp.ones((1, inputs), jnp.float32), jnp.zeros((2, inputs), jnp.float32)], axis=0
    )
    vis, size, sums = first_iteration(arrived, mask, weight, freq)
    fitted = None
    for iteration in range(1, ITERS):
        sums, gains, fitted = next_iteration(
            gains, all_sum(sums, devices), mask, weight, freq, vis, size
        )
    totals = all_sum(sums, devices)
    gains = solve_update([gains[k : k + 1] for k in range(3)], [totals[k : k + 1] for k in range(6)])
    return (gains, fitted)


def solution(mesh):
    placed = (P(("groups", "chan"), None, None), P("groups"), P(("groups", "chan")))
    return jax.shard_map(
        local,
        mesh=mesh,
        in_specs=placed,
        out_specs=(P(None, "groups"), P(None, ("groups", "chan"), None)),
        check_vma=False,
    )
```

```python
import functools
import math

import jax
import jax.numpy as jnp
from jax import lax
from jax.experimental import pallas as pl
from jax.experimental.pallas import tpu as pltpu
from jax.sharding import PartitionSpec as P

ITERS = 3
TILE = 128
GROUP = 32
UNIT = 16
PARTS = 2
AHEAD = 1
HUGE = 1e38
VMEM_LIMIT = 16 * 1024 * 1024

huber_scale = 0.25
damping = 0.5


def solve_update(gains, sums):
    determinant = jnp.maximum(sums[3] * sums[5] - sums[4] * sums[4], 1.0)
    step_phase = (sums[5] * sums[1] - sums[4] * sums[2]) / determinant
    step_delay = (sums[3] * sums[2] - sums[4] * sums[1]) / determinant
    amplitude = gains[0] * (1.0 + damping * (sums[0] - sums[3]) / jnp.maximum(sums[3], 1.0))
    return jnp.concatenate(
        [amplitude, gains[1] + damping * step_phase, gains[2] + damping * step_delay], axis=0
    )


def solve_rows(gains, sums):
    bound = jnp.maximum(sums[3] * sums[5] - sums[4] * sums[4], 1.0)
    phase = (sums[5] * sums[1] - sums[4] * sums[2]) / bound
    delay = (sums[3] * sums[2] - sums[4] * sums[1]) / bound
    ratio = gains[0] * (sums[0] - sums[3]) / jnp.maximum(sums[3], 1.0)
    row = lax.broadcasted_iota(jnp.int32, gains.shape, 0)
    return gains + damping * jnp.where(row == 0, ratio, jnp.where(row == 1, phase, delay))


def rows_of(ref, count):
    return [ref[k : k + 1, :] for k in range(count)]


def places(tiles):
    out = {}
    for part, rows in enumerate(tile_parts(tiles)):
        pairs = [(ti, tj) for ti in rows for tj in range(ti, tiles)]
        out.update({pair: (part, k) for k, pair in enumerate(pairs)})
    return out


def part_size(tiles):
    return max(k for _, k in places(tiles).values()) + 1


def drain(jobs):
    for _ in jobs:
        pass


def pair_sums(c, rows, tiles, terms, ahead, cols_ref, rows_ref):
    for ti in rows:
        for first in range(0, TILE, GROUP):
            for _ in range(AHEAD):
                next(ahead, None)
            row = ti * TILE + first
            totals = [None] * (GROUP // UNIT)
            for tj in range(ti, tiles):
                parts = None
                for unit in range(GROUP // UNIT):
                    at = first + unit * UNIT
                    keep = None
                    if tj == ti:
                        ids = lax.broadcasted_iota(jnp.int32, (UNIT, TILE), 0) + at
                        keep = ids != lax.broadcasted_iota(jnp.int32, (UNIT, TILE), 1)
                    got = terms(ti, tj, at, keep)
                    if totals[unit] is None:
                        totals[unit] = got
                    else:
                        totals[unit] = [a + b for a, b in zip(totals[unit], got)]
                    if tj > ti:
                        part = [x.reshape(UNIT // 8, 8, TILE).sum(axis=0) for x in got]
                        parts = part if parts is None else [a + b for a, b in zip(parts, part)]
                if tj > ti:
                    lanes = slice(tj * TILE, (tj + 1) * TILE)
                    for k in range(3):
                        cols_ref[k, :, lanes] += parts[k] if k != 1 else -parts[k]
            for unit in range(GROUP // UNIT):
                fold_rows(c, row + unit * UNIT, totals[unit], rows_ref)
    drain(ahead)


def tile_parts(tiles):
    order = [r for p in range((tiles + 1) // 2) for r in sorted({p, tiles - 1 - p})]
    size = -(-len(order) // PARTS)
    return [order[k : k + size] for k in range(0, len(order), size)]


def fold_rows(c, row, totals, rows_ref):
    lanes = lax.broadcasted_iota(jnp.int32, (UNIT, TILE), 1)
    for k in range(3):
        total = jnp.broadcast_to(jnp.sum(totals[k], axis=1, keepdims=True), (UNIT, TILE))
        pltpu.store(rows_ref.at[row : row + UNIT, :], total, mask=lanes == 8 * k + c)


def store_cols(c, cols_ref, colsum_ref):
    for k in range(3):
        colsum_ref[c, k : k + 1, :] = jnp.sum(cols_ref[k], axis=0, keepdims=True)


def channel_totals(tiles, rows_ref, colsum_ref, scales):
    turned = [rows_ref[t * TILE : (t + 1) * TILE, :].T for t in range(tiles)]
    chans = colsum_ref.shape[0]
    return [
        scales[k]
        * (jnp.concatenate([t[8 * k : 8 * k + chans] for t in turned], axis=1) + colsum_ref[:, k, :])
        for k in range(3)
    ]


def store_sums(totals, weight, freq, sums_ref):
    prod_re, prod_im, curvature = totals
    wim = weight * prod_im
    wcu = weight * curvature
    sums_ref[...] = jnp.concatenate(
        [
            jnp.sum(x, axis=0, keepdims=True)
            for x in (weight * prod_re, wim, freq * wim, wcu, freq * wcu, freq * freq * wcu)
        ],
        axis=0,
    )


def first_kernel(mask_ref, weight_ref, freq_ref, x_ref, vis_ref, size_ref, sums_ref,
                 wide_ref, right_ref, left_ref, maskrow_ref, base_ref, ahead_ref, cols_ref,
                 rows_ref, colsum_ref):
    c = pl.program_id(0)
    inputs, chans, width = x_ref.shape
    tiles = inputs // TILE
    half = width // 2
    parts, place = tile_parts(tiles), places(tiles)
    last = chans - 1

    def load_channel(c):
        lanes = lax.broadcasted_iota(jnp.int32, (TILE, width), 1)
        slot = lax.rem(c, 2)
        for t in range(tiles):
            at = slice(t * TILE, (t + 1) * TILE)
            rows = wide_ref[pl.ds(t * TILE * chans + c, TILE, stride=chans), :]
            rows = rows * maskrow_ref[at, :]
            right_ref[slot, at, :] = rows.astype(jnp.bfloat16)
            rows = rows + rows
            turned = pltpu.roll(rows, half, 1)
            left_ref[slot, t, :TILE, :] = rows.astype(jnp.bfloat16)
            left_ref[slot, t, TILE:, :] = jnp.where(lanes < half, turned, -turned).astype(jnp.bfloat16)

    def correlate(c, part):
        slot = lax.rem(c, 2)
        for ti in parts[part]:
            yield
            twice = lax.dot_general(
                left_ref[slot, ti], right_ref[slot, ti * TILE :, :], (((1,), (1,)), ((), ())),
                preferred_element_type=jnp.float32,
            ).astype(jnp.bfloat16)
            for tj in range(ti, tiles):
                at = slice((tj - ti) * TILE, (tj - ti + 1) * TILE)
                place_part, k = place[ti, tj]
                for p in (0, 1):
                    value = twice[p * TILE : (p + 1) * TILE, at]
                    if place_part == 0:
                        ahead_ref[k, p] = value
                    else:
                        vis_ref[c, place_part, k, p] = value

    @pl.when(c == 0)
    def _():
        rows_ref[...] = jnp.zeros_like(rows_ref)
        for t in range(tiles):
            at = slice(t * TILE, (t + 1) * TILE)
            block = x_ref[at].astype(jnp.float32)
            wide_ref[pl.ds(t * TILE * chans, TILE * chans), :] = block.reshape(TILE * chans, width)
            maskrow_ref[at, :] = jnp.broadcast_to(mask_ref[:, at] * 0.125, (TILE, TILE)).T
        flagged = (1.0 - mask_ref[...]) * HUGE
        ones = jnp.ones_like(flagged)
        sub = lax.broadcasted_iota(jnp.int32, (16, inputs), 0)
        near = jnp.where(sub == 0, 5.0 * ones, jnp.where(sub == 1, flagged, jnp.where(sub == 2, ones, 0.0)))
        far = jnp.where(sub < 2, ones, jnp.where(sub == 2, flagged, 0.0))
        near, far = near.astype(jnp.bfloat16), far.astype(jnp.bfloat16)
        for ti in range(tiles):
            base = lax.dot_general(
                near[:, ti * TILE : (ti + 1) * TILE], far[:, ti * TILE :], (((0,), (0,)), ((), ())),
                preferred_element_type=jnp.float32,
            )
            for tj in range(ti, tiles):
                base_ref[place[ti, tj]] = base[:, (tj - ti) * TILE : (tj - ti + 1) * TILE]

    @pl.when(c == 0)
    def _():
        load_channel(c)

    @pl.when(c == 0)
    def _():
        drain(correlate(c, 0))

    def terms(ti, tj, first, keep):
        rows = slice(first, first + UNIT)
        part, k = place[ti, tj]
        vis = []
        for p in (0, 1):
            if part == 0:
                value = ahead_ref[k, p, rows, :]
                vis_ref[c, part, k, p, rows, :] = value
            else:
                value = vis_ref[c, part, k, p, rows, :]
            vis.append(value.astype(jnp.float32))
        size = vis[0] * vis[0] + vis[1] * vis[1]
        size_ref[c, part, k, rows, :] = size + 1.0
        robust = 1.0 / (size + (base_ref[part, k, rows, :] - 4.0 * vis[0]))
        if keep is not None:
            robust = jnp.where(keep, robust, 0.0)
        return [robust * vis[0], robust * vis[1], robust]

    for part in range(len(parts)):
        @pl.when(c >= -part)
        def _(part=part):
            if part == 0:
                cols_ref[...] = jnp.zeros_like(cols_ref)
            if part + 1 < len(parts):
                ahead = correlate(c, part + 1)
            else:
                ahead = correlate(jnp.minimum(c + 1, last), 0)
            if part == 0:
                load_channel(jnp.minimum(c + 1, last))
            pair_sums(c, parts[part], tiles, terms, ahead, cols_ref, rows_ref)
            if part + 1 == len(parts):
                store_cols(c, cols_ref, colsum_ref)

    @pl.when(c == last)
    def _():
        totals = channel_totals(tiles, rows_ref, colsum_ref, (0.5, 0.5, 1.0))
        store_sums(totals, weight_ref[...], freq_ref[...], sums_ref)


def pieces(value):
    out = []
    for _ in range(3):
        out.append(value.astype(jnp.bfloat16).astype(jnp.float32))
        value = value - out[-1]
    return out


def next_kernel(ways, gains_ref, mask_ref, weight_ref, freq_ref, vis_ref, size_ref, *refs):
    old_refs = refs[:ways]
    (sums_ref, new_ref, fit_ref, model_ref, pair_ref, square_ref, left_ref, right_ref, cols_ref,
     rows_ref, colsum_ref) = refs[ways:]
    c = pl.program_id(0)
    last = pl.num_programs(0) - 1
    inputs = mask_ref.shape[1]
    tiles = inputs // TILE
    parts, place = tile_parts(tiles), places(tiles)
    sub = lax.broadcasted_iota(jnp.int32, (8, inputs), 0)
    zero = jnp.zeros((8, inputs), jnp.float32)

    def spread(piece, count):
        return jnp.broadcast_to(piece, (count, inputs))

    def load_channel(c):
        slot = lax.rem(c, 2)
        for p in (0, 1):
            own = model_ref[c, 8 * p : 8 * p + 8, :]
            own = jnp.concatenate([own] * 3 + [zero], axis=0).astype(jnp.bfloat16)
            for t in range(tiles):
                left_ref[slot, t, :, p * TILE : (p + 1) * TILE] = own[:, t * TILE : (t + 1) * TILE]
        right = [
            jnp.where(sub < 3, spread(model_ref[c, k : k + 1, :], 8), spread(model_ref[c, 3 + k : 4 + k, :], 8))
            for k in range(3)
        ]
        right_ref[slot] = jnp.concatenate(right + [zero], axis=0).astype(jnp.bfloat16)

    def model(c, part):
        slot = lax.rem(c, 2)
        for ti in parts[part]:
            yield
            pair = lax.dot_general(
                left_ref[slot, ti], right_ref[slot, :, ti * TILE :], (((0,), (0,)), ((), ())),
                preferred_element_type=jnp.float32,
            )
            for tj in range(ti, tiles):
                at = slice((tj - ti) * TILE, (tj - ti + 1) * TILE)
                for p in (0, 1):
                    pair_ref[place[ti, tj] + (p,)] = pair[p * TILE : (p + 1) * TILE, at]

    @pl.when(c == 0)
    def _():
        rows_ref[...] = jnp.zeros_like(rows_ref)
        old = add_up([ref[...] for ref in old_refs])
        gains = solve_update(rows_of(gains_ref, 3), [old[k : k + 1, :] for k in range(6)])
        new_ref[...] = gains
        angles = gains[1:2] + freq_ref[...] * gains[2:3]
        amplitude = gains[0:1] * mask_ref[...]
        double = amplitude + amplitude
        model_re = pieces(double * jnp.cos(angles))
        model_im = pieces(double * jnp.sin(angles))
        for k in range(3):
            model_ref[:, k, :] = model_re[k]
            model_ref[:, 3 + k, :] = model_im[k]
            model_ref[:, 8 + k, :] = model_im[k]
            model_ref[:, 11 + k, :] = -model_re[k]
        for k in (6, 7, 14, 15):
            model_ref[:, k, :] = jnp.zeros_like(angles)
        b = pieces(double * amplitude)
        b = [jnp.broadcast_to(x, (8, inputs)) for x in b]
        left = jnp.where(sub < 3, b[0], jnp.where(sub < 5, b[1], jnp.where(sub < 6, b[2], 0.0)))
        right = jnp.where(
            (sub == 0) | (sub == 3) | (sub == 5), b[0], jnp.where((sub == 1) | (sub == 4), b[1], b[2])
        )
        left = jnp.concatenate([left, zero], axis=0).astype(jnp.bfloat16)
        right = jnp.concatenate([right, zero], axis=0).astype(jnp.bfloat16)
        for ti in range(tiles):
            square = lax.dot_general(
                left[:, ti * TILE : (ti + 1) * TILE], right[:, ti * TILE :], (((0,), (0,)), ((), ())),
                preferred_element_type=jnp.float32,
            )
            for tj in range(ti, tiles):
                square_ref[place[ti, tj]] = square[:, (tj - ti) * TILE : (tj - ti + 1) * TILE]

    @pl.when(c == 0)
    def _():
        load_channel(c)
        drain(model(c, 0))

    def terms(ti, tj, first, keep):
        part, k = place[ti, tj]
        rows = slice(first, first + UNIT)
        vis_re, vis_im = [vis_ref[c, part, k, p, rows, :].astype(jnp.float32) for p in (0, 1)]
        pair_re, pair_im = [pair_ref[part, k, p, rows, :] for p in (0, 1)]
        square = square_ref[part, k, rows, :]
        prod_re = vis_re * pair_re + vis_im * pair_im
        prod_im = vis_im * pair_re - vis_re * pair_im
        robust = 1.0 / (size_ref[c, part, k, rows, :] - prod_re + square)
        if keep is not None:
            robust = jnp.where(keep, robust, 0.0)
        return [robust * prod_re, robust * prod_im, robust * square]

    for part in range(len(parts)):
        @pl.when(c >= -part)
        def _(part=part):
            if part == 0:
                cols_ref[...] = jnp.zeros_like(cols_ref)
            if part + 1 < len(parts):
                ahead = model(c, part + 1)
            else:
                ahead = model(jnp.minimum(c + 1, last), 0)
            if part == 0:
                load_channel(jnp.minimum(c + 1, last))
            pair_sums(c, parts[part], tiles, terms, ahead, cols_ref, rows_ref)
            if part + 1 == len(parts):
                store_cols(c, cols_ref, colsum_ref)

    @pl.when(c == last)
    def _():
        totals = channel_totals(tiles, rows_ref, colsum_ref, (0.125, 0.125, 0.25))
        store_sums(totals, weight_ref[...], freq_ref[...], sums_ref)
        bound = jnp.maximum(totals[2], 1.0)
        fit_ref[0] = totals[0] / bound
        fit_ref[1] = totals[1] / bound


def whole(shape):
    return pl.BlockSpec(shape, lambda c: (0,) * len(shape))


RESIDENT = pl.BlockSpec(memory_space=pltpu.VMEM)


def held(x):
    return pltpu.with_memory_space_constraint(x, pltpu.VMEM)


def split_kernel(volt_ref, out_ref, sems):
    devices, _, chans, _ = out_ref.shape
    copies = [
        pltpu.make_async_copy(volt_ref.at[:, d * chans : (d + 1) * chans, :], out_ref.at[d], sems.at[d])
        for d in range(devices)
    ]
    for copy in copies:
        copy.start()
    for copy in copies:
        copy.wait()


def split_channels(voltages, devices):
    inputs_dev, channels, width = voltages.shape
    return pl.pallas_call(
        split_kernel,
        in_specs=[pl.BlockSpec(memory_space=pltpu.HBM)],
        out_specs=pl.BlockSpec(memory_space=pl.ANY),
        out_shape=jax.ShapeDtypeStruct(
            (devices, inputs_dev, channels // devices, width), voltages.dtype
        ),
        scratch_shapes=[pltpu.SemaphoreType.DMA((devices,))],
        name="split_channels",
    )(pltpu.with_memory_space_constraint(voltages, pltpu.HBM))


def first_iteration(x, mask, weight, freq):
    inputs, chans, width = x.shape
    tiles = inputs // TILE
    steps, size = len(tile_parts(tiles)), part_size(tiles)
    return pl.pallas_call(
        first_kernel,
        grid=(chans,),
        in_specs=[whole(mask.shape), whole(weight.shape), whole(freq.shape), whole(x.shape)],
        out_specs=[RESIDENT, RESIDENT, whole((6, inputs))],
        out_shape=[
            pltpu.VMEM((chans, steps, size, 2, TILE, TILE), jnp.bfloat16),
            pltpu.VMEM((chans, steps, size, TILE, TILE), jnp.float32),
            jax.ShapeDtypeStruct((6, inputs), jnp.float32),
        ],
        scratch_shapes=[
            pltpu.VMEM((inputs * chans, width), jnp.float32),
            pltpu.VMEM((2, inputs, width), jnp.bfloat16),
            pltpu.VMEM((2, tiles, 2 * TILE, width), jnp.bfloat16),
            pltpu.VMEM((inputs, TILE), jnp.float32),
            pltpu.VMEM((steps, size, TILE, TILE), jnp.float32),
            pltpu.VMEM((size, 2, TILE, TILE), jnp.bfloat16),
            pltpu.VMEM((3, 8, inputs), jnp.float32),
            pltpu.VMEM((inputs, TILE), jnp.float32),
            pltpu.VMEM((chans, 8, inputs), jnp.float32),
        ],
        compiler_params=pltpu.CompilerParams(vmem_limit_bytes=VMEM_LIMIT),
        name="first_iteration",
    )(mask, weight, freq, x)


def next_iteration(gains, old_sums, mask, weight, freq, vis, size):
    chans, steps, count = size.shape[:3]
    inputs = mask.shape[1]
    tiles = inputs // TILE
    return pl.pallas_call(
        functools.partial(next_kernel, len(old_sums)),
        grid=(chans,),
        in_specs=[whole(gains.shape), whole(mask.shape), whole(weight.shape), whole(freq.shape)]
        + [RESIDENT, RESIDENT] + [whole((6, inputs)) for _ in old_sums],
        out_specs=[whole((6, inputs)), whole((3, inputs)), whole((2, chans, inputs))],
        out_shape=[
            jax.ShapeDtypeStruct((6, inputs), jnp.float32),
            jax.ShapeDtypeStruct((3, inputs), jnp.float32),
            jax.ShapeDtypeStruct((2, chans, inputs), jnp.float32),
        ],
        scratch_shapes=[
            pltpu.VMEM((chans, 16, inputs), jnp.float32),
            pltpu.VMEM((steps, count, 2, TILE, TILE), jnp.float32),
            pltpu.VMEM((steps, count, TILE, TILE), jnp.float32),
            pltpu.VMEM((2, tiles, 32, 2 * TILE), jnp.bfloat16),
            pltpu.VMEM((2, 32, inputs), jnp.bfloat16),
            pltpu.VMEM((3, 8, inputs), jnp.float32),
            pltpu.VMEM((inputs, TILE), jnp.float32),
            pltpu.VMEM((chans, 8, inputs), jnp.float32),
        ],
        compiler_params=pltpu.CompilerParams(vmem_limit_bytes=VMEM_LIMIT),
        name="next_iteration",
    )(gains, mask, weight, freq, held(vis), held(size), *old_sums)


def add_up(parts):
    while len(parts) > 1:
        parts = [a + b for a, b in zip(parts[::2], parts[1::2])]
    return parts[0]


def all_sum(part, devices):
    if devices & (devices - 1):
        return [lax.psum(part, "chan")]
    reach = 1
    while reach < devices:
        ways = 4 if devices // reach >= 4 else 2
        got = [part] + [
            lax.ppermute(part, "chan", [(i, i ^ (k * reach)) for i in range(devices)])
            for k in range(1, ways)
        ]
        reach *= ways
        if reach == devices:
            return got
        part = add_up(got)
    return [part]


def local(voltages, antenna_usable_mask, channel_flags):
    devices = lax.axis_size("chan")
    inputs_dev, channels, sample_cols = voltages.shape
    chan_dev = channels // devices
    blocks = split_channels(voltages, devices)
    turned = lax.all_to_all(blocks, "chan", split_axis=0, concat_axis=0, tiled=True)
    inputs = inputs_dev * devices
    arrived = turned.reshape(inputs, chan_dev, sample_cols)
    first_channel = lax.axis_index("chan") * chan_dev
    channel_ids = (first_channel + jnp.arange(chan_dev)).astype(jnp.float32)
    freq = (2.0 * math.pi * (channel_ids + 0.5) / (chan_dev * devices))[:, None]
    weight = channel_flags.astype(jnp.float32)[:, None]
    mask = antenna_usable_mask.astype(jnp.float32)[None, :]
    gains = jnp.concatenate(
        [jnp.ones((1, inputs), jnp.float32), jnp.zeros((2, inputs), jnp.float32)], axis=0
    )
    vis, size, sums = first_iteration(arrived, mask, weight, freq)
    fitted = None
    for iteration in range(1, ITERS):
        sums, gains, fitted = next_iteration(
            gains, all_sum(sums, devices), mask, weight, freq, vis, size
        )
    totals = add_up(all_sum(sums, devices))
    gains = solve_rows(gains, totals)
    return (gains, fitted)


def solution(mesh):
    placed = (P(("groups", "chan"), None, None), P("groups"), P(("groups", "chan")))
    return jax.shard_map(
        local,
        mesh=mesh,
        in_specs=placed,
        out_specs=(P(None, "groups"), P(None, ("groups", "chan"), None)),
        check_vma=False,
    )
```

```python
import functools
import itertools
import math

import jax
import jax.numpy as jnp
from jax import lax
from jax.experimental import pallas as pl
from jax.experimental.pallas import tpu as pltpu
from jax.sharding import PartitionSpec as P

ITERS = 3
TILE = 128
UNIT = 16
PARTS = 2
HUGE = 1e38
VMEM_LIMIT = 16 * 1024 * 1024

huber_scale = 0.25
damping = 0.5


def solve_update(gains, sums):
    determinant = jnp.maximum(sums[3] * sums[5] - sums[4] * sums[4], 1.0)
    step_phase = (sums[5] * sums[1] - sums[4] * sums[2]) / determinant
    step_delay = (sums[3] * sums[2] - sums[4] * sums[1]) / determinant
    amplitude = gains[0] * (1.0 + damping * (sums[0] - sums[3]) / jnp.maximum(sums[3], 1.0))
    return jnp.concatenate(
        [amplitude, gains[1] + damping * step_phase, gains[2] + damping * step_delay], axis=0
    )


def solve_rows(gains, sums):
    bound = jnp.maximum(sums[3] * sums[5] - sums[4] * sums[4], 1.0)
    phase = (sums[5] * sums[1] - sums[4] * sums[2]) / bound
    delay = (sums[3] * sums[2] - sums[4] * sums[1]) / bound
    ratio = gains[0] * (sums[0] - sums[3]) / jnp.maximum(sums[3], 1.0)
    row = lax.broadcasted_iota(jnp.int32, gains.shape, 0)
    return gains + damping * jnp.where(row == 0, ratio, jnp.where(row == 1, phase, delay))


def rows_of(ref, count):
    return [ref[k : k + 1, :] for k in range(count)]


def places(tiles):
    out = {}
    for part, rows in enumerate(tile_parts(tiles)):
        pairs = [(ti, tj) for ti in rows for tj in range(ti, tiles)]
        out.update({pair: (part, k) for k, pair in enumerate(pairs)})
    return out


def part_size(tiles):
    return max(k for _, k in places(tiles).values()) + 1


def drain(jobs):
    for _ in jobs:
        pass


def pair_sums(c, rows, tiles, group, terms, ahead, cols_ref, rows_ref):
    for ti in rows:
        for first in range(0, TILE, group):
            for _ in range(1 + group // 64):
                next(ahead, None)
            row = ti * TILE + first
            totals = [None] * (group // UNIT)
            for tj in range(ti, tiles):
                parts = None
                for unit in range(group // UNIT):
                    at = first + unit * UNIT
                    keep = None
                    if tj == ti:
                        ids = lax.broadcasted_iota(jnp.int32, (UNIT, TILE), 0) + at
                        keep = ids != lax.broadcasted_iota(jnp.int32, (UNIT, TILE), 1)
                    got = terms(ti, tj, at, keep)
                    if totals[unit] is None:
                        totals[unit] = got
                    else:
                        totals[unit] = [a + b for a, b in zip(totals[unit], got)]
                    if tj > ti:
                        part = [x.reshape(UNIT // 8, 8, TILE).sum(axis=0) for x in got]
                        parts = part if parts is None else [a + b for a, b in zip(parts, part)]
                if tj > ti:
                    lanes = slice(tj * TILE, (tj + 1) * TILE)
                    for k in range(3):
                        cols_ref[k, :, lanes] += parts[k] if k != 1 else -parts[k]
            for unit in range(group // UNIT):
                fold_rows(c, row + unit * UNIT, totals[unit], rows_ref)
    drain(ahead)


def tile_parts(tiles):
    order = [r for p in range((tiles + 1) // 2) for r in sorted({p, tiles - 1 - p})]
    size = -(-len(order) // PARTS)
    return [order[k : k + size] for k in range(0, len(order), size)]


def fold_rows(c, row, totals, rows_ref):
    lanes = lax.broadcasted_iota(jnp.int32, (UNIT, TILE), 1)
    for k in range(3):
        total = jnp.broadcast_to(jnp.sum(totals[k], axis=1, keepdims=True), (UNIT, TILE))
        pltpu.store(rows_ref.at[row : row + UNIT, :], total, mask=lanes == 8 * k + c)


def store_cols(c, cols_ref, colsum_ref):
    for k in range(3):
        colsum_ref[c, k : k + 1, :] = jnp.sum(cols_ref[k], axis=0, keepdims=True)


def channel_totals(tiles, rows_ref, colsum_ref, scales):
    turned = [rows_ref[t * TILE : (t + 1) * TILE, :].T for t in range(tiles)]
    chans = colsum_ref.shape[0]
    return [
        scales[k]
        * (jnp.concatenate([t[8 * k : 8 * k + chans] for t in turned], axis=1) + colsum_ref[:, k, :])
        for k in range(3)
    ]


def store_sums(totals, weight, freq, sums_ref):
    prod_re, prod_im, curvature = totals
    wim = weight * prod_im
    wcu = weight * curvature
    sums_ref[...] = jnp.concatenate(
        [
            jnp.sum(x, axis=0, keepdims=True)
            for x in (weight * prod_re, wim, freq * wim, wcu, freq * wcu, freq * freq * wcu)
        ],
        axis=0,
    )


def first_kernel(mask_ref, weight_ref, freq_ref, arrived_ref, vis_ref, size_ref, sums_ref, x_ref, sem,
                 wide_ref, right_ref, left_ref, maskrow_ref, base_ref, ahead_ref, cols_ref,
                 rows_ref, colsum_ref):
    c = pl.program_id(0)
    inputs, chans, width = x_ref.shape
    tiles = inputs // TILE
    half = width // 2
    parts, place = tile_parts(tiles), places(tiles)
    last = chans - 1

    def load_channel(c):
        lanes = lax.broadcasted_iota(jnp.int32, (TILE, width), 1)
        slot = lax.rem(c, 2)
        for t in range(tiles):
            yield
            at = slice(t * TILE, (t + 1) * TILE)
            rows = wide_ref[pl.ds(t * TILE * chans + c, TILE, stride=chans), :]
            rows = rows * maskrow_ref[at, :]
            right_ref[slot, at, :] = rows.astype(jnp.bfloat16)
            rows = rows + rows
            turned = pltpu.roll(rows, half, 1)
            left_ref[slot, t, :TILE, :] = rows.astype(jnp.bfloat16)
            left_ref[slot, t, TILE:, :] = jnp.where(lanes < half, turned, -turned).astype(jnp.bfloat16)

    def correlate(c, part):
        slot = lax.rem(c, 2)
        for ti in parts[part]:
            yield
            twice = lax.dot_general(
                left_ref[slot, ti], right_ref[slot, ti * TILE :, :], (((1,), (1,)), ((), ())),
                preferred_element_type=jnp.float32,
            ).astype(jnp.bfloat16)
            for tj in range(ti, tiles):
                at = slice((tj - ti) * TILE, (tj - ti + 1) * TILE)
                place_part, k = place[ti, tj]
                for p in (0, 1):
                    value = twice[p * TILE : (p + 1) * TILE, at]
                    if place_part == 0:
                        ahead_ref[k, p] = value
                    else:
                        vis_ref[c, place_part, k, p] = value

    @pl.when(c == 0)
    def _():
        copy = pltpu.make_async_copy(arrived_ref, x_ref, sem)
        copy.start()
        rows_ref[...] = jnp.zeros_like(rows_ref)
        copy.wait()
        for t in range(tiles):
            at = slice(t * TILE, (t + 1) * TILE)
            block = x_ref[at].astype(jnp.float32)
            wide_ref[pl.ds(t * TILE * chans, TILE * chans), :] = block.reshape(TILE * chans, width)
            maskrow_ref[at, :] = jnp.broadcast_to(mask_ref[:, at] * 0.125, (TILE, TILE)).T
        flagged = (1.0 - mask_ref[...]) * HUGE
        ones = jnp.ones_like(flagged)
        sub = lax.broadcasted_iota(jnp.int32, (16, inputs), 0)
        near = jnp.where(sub == 0, 5.0 * ones, jnp.where(sub == 1, flagged, jnp.where(sub == 2, ones, 0.0)))
        far = jnp.where(sub < 2, ones, jnp.where(sub == 2, flagged, 0.0))
        near, far = near.astype(jnp.bfloat16), far.astype(jnp.bfloat16)
        for ti in range(tiles):
            base = lax.dot_general(
                near[:, ti * TILE : (ti + 1) * TILE], far[:, ti * TILE :], (((0,), (0,)), ((), ())),
                preferred_element_type=jnp.float32,
            )
            for tj in range(ti, tiles):
                base_ref[place[ti, tj]] = base[:, (tj - ti) * TILE : (tj - ti + 1) * TILE]

    @pl.when(c == 0)
    def _():
        drain(load_channel(c))

    @pl.when(c == 0)
    def _():
        drain(correlate(c, 0))

    def terms(ti, tj, first, keep):
        rows = slice(first, first + UNIT)
        part, k = place[ti, tj]
        vis = []
        for p in (0, 1):
            if part == 0:
                value = ahead_ref[k, p, rows, :]
                vis_ref[c, part, k, p, rows, :] = value
            else:
                value = vis_ref[c, part, k, p, rows, :]
            vis.append(value.astype(jnp.float32))
        size = vis[0] * vis[0] + vis[1] * vis[1]
        size_ref[c, part, k, rows, :] = size + 1.0
        robust = 1.0 / (size + (base_ref[part, k, rows, :] - 4.0 * vis[0]))
        if keep is not None:
            robust = jnp.where(keep, robust, 0.0)
        return [robust * vis[0], robust * vis[1], robust]

    for part in range(len(parts)):
        @pl.when(c >= -part)
        def _(part=part):
            if part == 0:
                cols_ref[...] = jnp.zeros_like(cols_ref)
            if part + 1 < len(parts):
                ahead = correlate(c, part + 1)
            else:
                ahead = correlate(jnp.minimum(c + 1, last), 0)
            if part == 0:
                ahead = itertools.chain(ahead, load_channel(jnp.minimum(c + 1, last)))
            pair_sums(c, parts[part], tiles, TILE, terms, ahead, cols_ref, rows_ref)
            if part + 1 == len(parts):
                store_cols(c, cols_ref, colsum_ref)

    @pl.when(c == last)
    def _():
        totals = channel_totals(tiles, rows_ref, colsum_ref, (0.5, 0.5, 1.0))
        store_sums(totals, weight_ref[...], freq_ref[...], sums_ref)


def pieces(value):
    out = []
    for _ in range(3):
        out.append(value.astype(jnp.bfloat16).astype(jnp.float32))
        value = value - out[-1]
    return out


def next_kernel(ways, gains_ref, mask_ref, weight_ref, freq_ref, vis_ref, size_ref, *refs):
    old_refs = refs[:ways]
    (sums_ref, new_ref, fit_ref, model_ref, pair_ref, square_ref, left_ref, right_ref, cols_ref,
     rows_ref, colsum_ref) = refs[ways:]
    c = pl.program_id(0)
    last = pl.num_programs(0) - 1
    inputs = mask_ref.shape[1]
    tiles = inputs // TILE
    parts, place = tile_parts(tiles), places(tiles)
    sub = lax.broadcasted_iota(jnp.int32, (8, inputs), 0)
    zero = jnp.zeros((8, inputs), jnp.float32)

    def spread(piece, count):
        return jnp.broadcast_to(piece, (count, inputs))

    def load_channel(c):
        yield
        slot = lax.rem(c, 2)
        for p in (0, 1):
            own = model_ref[c, 8 * p : 8 * p + 8, :]
            own = jnp.concatenate([own] * 3 + [zero], axis=0).astype(jnp.bfloat16)
            for t in range(tiles):
                left_ref[slot, t, :, p * TILE : (p + 1) * TILE] = own[:, t * TILE : (t + 1) * TILE]
        right = [
            jnp.where(sub < 3, spread(model_ref[c, k : k + 1, :], 8), spread(model_ref[c, 3 + k : 4 + k, :], 8))
            for k in range(3)
        ]
        right_ref[slot] = jnp.concatenate(right + [zero], axis=0).astype(jnp.bfloat16)

    def model(c, part):
        slot = lax.rem(c, 2)
        for ti in parts[part]:
            yield
            pair = lax.dot_general(
                left_ref[slot, ti], right_ref[slot, :, ti * TILE :], (((0,), (0,)), ((), ())),
                preferred_element_type=jnp.float32,
            )
            for tj in range(ti, tiles):
                at = slice((tj - ti) * TILE, (tj - ti + 1) * TILE)
                for p in (0, 1):
                    pair_ref[place[ti, tj] + (p,)] = pair[p * TILE : (p + 1) * TILE, at]

    @pl.when(c == 0)
    def _():
        rows_ref[...] = jnp.zeros_like(rows_ref)
        old = add_up([ref[...] for ref in old_refs])
        gains = solve_update(rows_of(gains_ref, 3), [old[k : k + 1, :] for k in range(6)])
        new_ref[...] = gains
        angles = gains[1:2] + freq_ref[...] * gains[2:3]
        amplitude = gains[0:1] * mask_ref[...]
        double = amplitude + amplitude
        model_re = pieces(double * jnp.cos(angles))
        model_im = pieces(double * jnp.sin(angles))
        for k in range(3):
            model_ref[:, k, :] = model_re[k]
            model_ref[:, 3 + k, :] = model_im[k]
            model_ref[:, 8 + k, :] = model_im[k]
            model_ref[:, 11 + k, :] = -model_re[k]
        for k in (6, 7, 14, 15):
            model_ref[:, k, :] = jnp.zeros_like(angles)
        b = pieces(double * amplitude)
        b = [jnp.broadcast_to(x, (8, inputs)) for x in b]
        left = jnp.where(sub < 3, b[0], jnp.where(sub < 5, b[1], jnp.where(sub < 6, b[2], 0.0)))
        right = jnp.where(
            (sub == 0) | (sub == 3) | (sub == 5), b[0], jnp.where((sub == 1) | (sub == 4), b[1], b[2])
        )
        left = jnp.concatenate([left, zero], axis=0).astype(jnp.bfloat16)
        right = jnp.concatenate([right, zero], axis=0).astype(jnp.bfloat16)
        for ti in range(tiles):
            square = lax.dot_general(
                left[:, ti * TILE : (ti + 1) * TILE], right[:, ti * TILE :], (((0,), (0,)), ((), ())),
                preferred_element_type=jnp.float32,
            )
            for tj in range(ti, tiles):
                square_ref[place[ti, tj]] = square[:, (tj - ti) * TILE : (tj - ti + 1) * TILE]

    @pl.when(c == 0)
    def _():
        drain(load_channel(c))
        drain(model(c, 0))

    def terms(ti, tj, first, keep):
        part, k = place[ti, tj]
        rows = slice(first, first + UNIT)
        vis_re, vis_im = [vis_ref[c, part, k, p, rows, :].astype(jnp.float32) for p in (0, 1)]
        pair_re, pair_im = [pair_ref[part, k, p, rows, :] for p in (0, 1)]
        square = square_ref[part, k, rows, :]
        prod_re = vis_re * pair_re + vis_im * pair_im
        prod_im = vis_im * pair_re - vis_re * pair_im
        robust = 1.0 / (size_ref[c, part, k, rows, :] - prod_re + square)
        if keep is not None:
            robust = jnp.where(keep, robust, 0.0)
        return [robust * prod_re, robust * prod_im, robust * square]

    for part in range(len(parts)):
        @pl.when(c >= -part)
        def _(part=part):
            if part == 0:
                cols_ref[...] = jnp.zeros_like(cols_ref)
            if part + 1 < len(parts):
                ahead = model(c, part + 1)
            else:
                ahead = model(jnp.minimum(c + 1, last), 0)
            if part == 0:
                ahead = itertools.chain(ahead, load_channel(jnp.minimum(c + 1, last)))
            pair_sums(c, parts[part], tiles, 32, terms, ahead, cols_ref, rows_ref)
            if part + 1 == len(parts):
                store_cols(c, cols_ref, colsum_ref)

    @pl.when(c == last)
    def _():
        totals = channel_totals(tiles, rows_ref, colsum_ref, (0.125, 0.125, 0.25))
        store_sums(totals, weight_ref[...], freq_ref[...], sums_ref)
        bound = jnp.maximum(totals[2], 1.0)
        fit_ref[0] = totals[0] / bound
        fit_ref[1] = totals[1] / bound


def whole(shape):
    return pl.BlockSpec(shape, lambda c: (0,) * len(shape))


RESIDENT = pl.BlockSpec(memory_space=pltpu.VMEM)


def held(x):
    return pltpu.with_memory_space_constraint(x, pltpu.VMEM)


def split_kernel(volt_ref, out_ref):
    devices, _, chans, _ = out_ref.shape
    for d in range(devices):
        out_ref[d] = volt_ref[:, d * chans : (d + 1) * chans, :]


def split_channels(voltages, devices):
    inputs_dev, channels, width = voltages.shape
    chans, rows = channels // devices, max(inputs_dev // 2, 1)
    return pl.pallas_call(
        split_kernel,
        grid=(inputs_dev // rows,),
        in_specs=[pl.BlockSpec((rows, channels, width), lambda i: (i, 0, 0))],
        out_specs=pl.BlockSpec((devices, rows, chans, width), lambda i: (0, i, 0, 0)),
        out_shape=jax.ShapeDtypeStruct((devices, inputs_dev, chans, width), voltages.dtype),
        compiler_params=pltpu.CompilerParams(vmem_limit_bytes=VMEM_LIMIT),
        name="split_channels",
    )(voltages)


def first_iteration(x, mask, weight, freq):
    inputs, chans, width = x.shape
    tiles = inputs // TILE
    steps, size = len(tile_parts(tiles)), part_size(tiles)
    return pl.pallas_call(
        first_kernel,
        grid=(chans,),
        in_specs=[whole(mask.shape), whole(weight.shape), whole(freq.shape),
                  pl.BlockSpec(memory_space=pl.ANY)],
        out_specs=[RESIDENT, RESIDENT, whole((6, inputs))],
        out_shape=[
            pltpu.VMEM((chans, steps, size, 2, TILE, TILE), jnp.bfloat16),
            pltpu.VMEM((chans, steps, size, TILE, TILE), jnp.float32),
            jax.ShapeDtypeStruct((6, inputs), jnp.float32),
        ],
        scratch_shapes=[
            pltpu.VMEM((inputs, chans, width), x.dtype),
            pltpu.SemaphoreType.DMA,
            pltpu.VMEM((inputs * chans, width), jnp.float32),
            pltpu.VMEM((2, inputs, width), jnp.bfloat16),
            pltpu.VMEM((2, tiles, 2 * TILE, width), jnp.bfloat16),
            pltpu.VMEM((inputs, TILE), jnp.float32),
            pltpu.VMEM((steps, size, TILE, TILE), jnp.float32),
            pltpu.VMEM((size, 2, TILE, TILE), jnp.bfloat16),
            pltpu.VMEM((3, 8, inputs), jnp.float32),
            pltpu.VMEM((inputs, TILE), jnp.float32),
            pltpu.VMEM((chans, 8, inputs), jnp.float32),
        ],
        compiler_params=pltpu.CompilerParams(vmem_limit_bytes=VMEM_LIMIT),
        name="first_iteration",
    )(mask, weight, freq, x)


def next_iteration(gains, old_sums, mask, weight, freq, vis, size):
    chans, steps, count = size.shape[:3]
    inputs = mask.shape[1]
    tiles = inputs // TILE
    return pl.pallas_call(
        functools.partial(next_kernel, len(old_sums)),
        grid=(chans,),
        in_specs=[whole(gains.shape), whole(mask.shape), whole(weight.shape), whole(freq.shape)]
        + [RESIDENT, RESIDENT] + [whole((6, inputs)) for _ in old_sums],
        out_specs=[whole((6, inputs)), whole((3, inputs)), whole((2, chans, inputs))],
        out_shape=[
            jax.ShapeDtypeStruct((6, inputs), jnp.float32),
            jax.ShapeDtypeStruct((3, inputs), jnp.float32),
            jax.ShapeDtypeStruct((2, chans, inputs), jnp.float32),
        ],
        scratch_shapes=[
            pltpu.VMEM((chans, 16, inputs), jnp.float32),
            pltpu.VMEM((steps, count, 2, TILE, TILE), jnp.float32),
            pltpu.VMEM((steps, count, TILE, TILE), jnp.float32),
            pltpu.VMEM((2, tiles, 32, 2 * TILE), jnp.bfloat16),
            pltpu.VMEM((2, 32, inputs), jnp.bfloat16),
            pltpu.VMEM((3, 8, inputs), jnp.float32),
            pltpu.VMEM((inputs, TILE), jnp.float32),
            pltpu.VMEM((chans, 8, inputs), jnp.float32),
        ],
        compiler_params=pltpu.CompilerParams(vmem_limit_bytes=VMEM_LIMIT),
        name="next_iteration",
    )(gains, mask, weight, freq, held(vis), held(size), *old_sums)


def add_up(parts):
    while len(parts) > 1:
        parts = [a + b for a, b in zip(parts[::2], parts[1::2])]
    return parts[0]


def all_sum(part, devices):
    if devices & (devices - 1):
        return [lax.psum(part, "chan")]
    reach = 1
    while reach < devices:
        ways = 4 if devices // reach >= 4 else 2
        got = [part] + [
            lax.ppermute(part, "chan", [(i, i ^ (k * reach)) for i in range(devices)])
            for k in range(1, ways)
        ]
        reach *= ways
        if reach == devices:
            return got
        part = add_up(got)
    return [part]


def local(voltages, antenna_usable_mask, channel_flags):
    devices = lax.axis_size("chan")
    inputs_dev, channels, sample_cols = voltages.shape
    chan_dev = channels // devices
    blocks = split_channels(voltages, devices)
    turned = lax.all_to_all(blocks, "chan", split_axis=0, concat_axis=0, tiled=True)
    inputs = inputs_dev * devices
    arrived = turned.reshape(inputs, chan_dev, sample_cols)
    first_channel = lax.axis_index("chan") * chan_dev
    channel_ids = (first_channel + jnp.arange(chan_dev)).astype(jnp.float32)
    freq = (2.0 * math.pi * (channel_ids + 0.5) / (chan_dev * devices))[:, None]
    weight = channel_flags.astype(jnp.float32)[:, None]
    mask = antenna_usable_mask.astype(jnp.float32)[None, :]
    gains = jnp.concatenate(
        [jnp.ones((1, inputs), jnp.float32), jnp.zeros((2, inputs), jnp.float32)], axis=0
    )
    vis, size, sums = first_iteration(arrived, mask, weight, freq)
    fitted = None
    for iteration in range(1, ITERS):
        sums, gains, fitted = next_iteration(
            gains, all_sum(sums, devices), mask, weight, freq, vis, size
        )
    totals = add_up(all_sum(sums, devices))
    gains = solve_rows(gains, totals)
    return (gains, fitted)


def solution(mesh):
    placed = (P(("groups", "chan"), None, None), P("groups"), P(("groups", "chan")))
    return jax.shard_map(
        local,
        mesh=mesh,
        in_specs=placed,
        out_specs=(P(None, "groups"), P(None, ("groups", "chan"), None)),
        check_vma=False,
    )
```

```python
import functools
import itertools
import math

import jax
import jax.numpy as jnp
from jax import lax
from jax.experimental import pallas as pl
from jax.experimental.pallas import tpu as pltpu
from jax.sharding import PartitionSpec as P

ITERS = 3
TILE = 128
UNIT = 16
PARTS = 2
HUGE = 1e38
VMEM_LIMIT = 16 * 1024 * 1024

huber_scale = 0.25
damping = 0.5


def solve_update(gains, sums):
    determinant = jnp.maximum(sums[3] * sums[5] - sums[4] * sums[4], 1.0)
    step_phase = (sums[5] * sums[1] - sums[4] * sums[2]) / determinant
    step_delay = (sums[3] * sums[2] - sums[4] * sums[1]) / determinant
    amplitude = gains[0] * (1.0 + damping * (sums[0] - sums[3]) / jnp.maximum(sums[3], 1.0))
    return jnp.concatenate(
        [amplitude, gains[1] + damping * step_phase, gains[2] + damping * step_delay], axis=0
    )


def solve_rows(gains, sums):
    bound = jnp.maximum(sums[3] * sums[5] - sums[4] * sums[4], 1.0)
    phase = (sums[5] * sums[1] - sums[4] * sums[2]) / bound
    delay = (sums[3] * sums[2] - sums[4] * sums[1]) / bound
    ratio = gains[0] * (sums[0] - sums[3]) / jnp.maximum(sums[3], 1.0)
    row = lax.broadcasted_iota(jnp.int32, gains.shape, 0)
    return gains + damping * jnp.where(row == 0, ratio, jnp.where(row == 1, phase, delay))


def rows_of(ref, count):
    return [ref[k : k + 1, :] for k in range(count)]


def places(tiles):
    out = {}
    for part, rows in enumerate(tile_parts(tiles)):
        pairs = [(ti, tj) for ti in rows for tj in range(ti, tiles)]
        out.update({pair: (part, k) for k, pair in enumerate(pairs)})
    return out


def part_size(tiles):
    return max(k for _, k in places(tiles).values()) + 1


def drain(jobs):
    for _ in jobs:
        pass


def pair_sums(c, rows, tiles, group, terms, ahead, cols_ref, rows_ref):
    for ti in rows:
        for first in range(0, TILE, group):
            for _ in range(1 + group // 64):
                next(ahead, None)
            row = ti * TILE + first
            totals = [None] * (group // UNIT)
            for tj in range(ti, tiles):
                parts = None
                for unit in range(group // UNIT):
                    at = first + unit * UNIT
                    keep = None
                    if tj == ti:
                        ids = lax.broadcasted_iota(jnp.int32, (UNIT, TILE), 0) + at
                        keep = ids != lax.broadcasted_iota(jnp.int32, (UNIT, TILE), 1)
                    got = terms(ti, tj, at, keep)
                    if totals[unit] is None:
                        totals[unit] = got
                    else:
                        totals[unit] = [a + b for a, b in zip(totals[unit], got)]
                    if tj > ti:
                        part = [x.reshape(UNIT // 8, 8, TILE).sum(axis=0) for x in got]
                        parts = part if parts is None else [a + b for a, b in zip(parts, part)]
                if tj > ti:
                    lanes = slice(tj * TILE, (tj + 1) * TILE)
                    for k in range(3):
                        cols_ref[k, :, lanes] += parts[k] if k != 1 else -parts[k]
            for unit in range(group // UNIT):
                fold_rows(c, row + unit * UNIT, totals[unit], rows_ref)
    drain(ahead)


def tile_parts(tiles):
    order = [r for p in range((tiles + 1) // 2) for r in sorted({p, tiles - 1 - p})]
    size = -(-len(order) // PARTS)
    return [order[k : k + size] for k in range(0, len(order), size)]


def fold_rows(c, row, totals, rows_ref):
    lanes = lax.broadcasted_iota(jnp.int32, (UNIT, TILE), 1)
    for k in range(3):
        total = jnp.broadcast_to(jnp.sum(totals[k], axis=1, keepdims=True), (UNIT, TILE))
        pltpu.store(rows_ref.at[row : row + UNIT, :], total, mask=lanes == 8 * k + c)


def store_cols(c, cols_ref, colsum_ref):
    for k in range(3):
        colsum_ref[c, k : k + 1, :] = jnp.sum(cols_ref[k], axis=0, keepdims=True)


def channel_totals(tiles, rows_ref, colsum_ref, scales):
    turned = [rows_ref[t * TILE : (t + 1) * TILE, :].T for t in range(tiles)]
    chans = colsum_ref.shape[0]
    return [
        scales[k]
        * (jnp.concatenate([t[8 * k : 8 * k + chans] for t in turned], axis=1) + colsum_ref[:, k, :])
        for k in range(3)
    ]


def store_sums(totals, weight, freq, sums_ref):
    prod_re, prod_im, curvature = totals
    wim = weight * prod_im
    wcu = weight * curvature
    sums_ref[...] = jnp.concatenate(
        [
            jnp.sum(x, axis=0, keepdims=True)
            for x in (weight * prod_re, wim, freq * wim, wcu, freq * wcu, freq * freq * wcu)
        ],
        axis=0,
    )


def first_kernel(mask_ref, weight_ref, freq_ref, arrived_ref, vis_ref, size_ref, sums_ref, x_ref, sem,
                 wide_ref, right_ref, left_ref, maskrow_ref, base_ref, ahead_ref, cols_ref,
                 rows_ref, colsum_ref):
    c = pl.program_id(0)
    inputs, chans, width = x_ref.shape
    tiles = inputs // TILE
    half = width // 2
    parts, place = tile_parts(tiles), places(tiles)
    last = chans - 1

    def load_channel(c):
        lanes = lax.broadcasted_iota(jnp.int32, (TILE, width), 1)
        slot = lax.rem(c, 2)
        for t in range(tiles):
            yield
            at = slice(t * TILE, (t + 1) * TILE)
            rows = wide_ref[pl.ds(t * TILE * chans + c, TILE, stride=chans), :]
            rows = rows * maskrow_ref[at, :]
            right_ref[slot, at, :] = rows.astype(jnp.bfloat16)
            rows = rows + rows
            turned = pltpu.roll(rows, half, 1)
            left_ref[slot, t, :TILE, :] = rows.astype(jnp.bfloat16)
            left_ref[slot, t, TILE:, :] = jnp.where(lanes < half, turned, -turned).astype(jnp.bfloat16)

    def correlate(c, part):
        slot = lax.rem(c, 2)
        for ti in parts[part]:
            yield
            twice = lax.dot_general(
                left_ref[slot, ti], right_ref[slot, ti * TILE :, :], (((1,), (1,)), ((), ())),
                preferred_element_type=jnp.float32,
            ).astype(jnp.bfloat16)
            for tj in range(ti, tiles):
                at = slice((tj - ti) * TILE, (tj - ti + 1) * TILE)
                place_part, k = place[ti, tj]
                for p in (0, 1):
                    value = twice[p * TILE : (p + 1) * TILE, at]
                    if place_part == 0:
                        ahead_ref[k, p] = value
                    else:
                        vis_ref[c, place_part, k, p] = value

    @pl.when(c == 0)
    def _():
        copy = pltpu.make_async_copy(arrived_ref, x_ref, sem)
        copy.start()
        rows_ref[...] = jnp.zeros_like(rows_ref)
        copy.wait()
        for t in range(tiles):
            at = slice(t * TILE, (t + 1) * TILE)
            block = x_ref[at].astype(jnp.float32)
            wide_ref[pl.ds(t * TILE * chans, TILE * chans), :] = block.reshape(TILE * chans, width)
            maskrow_ref[at, :] = jnp.broadcast_to(mask_ref[:, at] * 0.125, (TILE, TILE)).T
        flagged = (1.0 - mask_ref[...]) * HUGE
        ones = jnp.ones_like(flagged)
        sub = lax.broadcasted_iota(jnp.int32, (16, inputs), 0)
        near = jnp.where(sub == 0, 5.0 * ones, jnp.where(sub == 1, flagged, jnp.where(sub == 2, ones, 0.0)))
        far = jnp.where(sub < 2, ones, jnp.where(sub == 2, flagged, 0.0))
        near, far = near.astype(jnp.bfloat16), far.astype(jnp.bfloat16)
        for ti in range(tiles):
            base = lax.dot_general(
                near[:, ti * TILE : (ti + 1) * TILE], far[:, ti * TILE :], (((0,), (0,)), ((), ())),
                preferred_element_type=jnp.float32,
            )
            for tj in range(ti, tiles):
                base_ref[place[ti, tj]] = base[:, (tj - ti) * TILE : (tj - ti + 1) * TILE]

    @pl.when(c == 0)
    def _():
        drain(load_channel(c))

    @pl.when(c == 0)
    def _():
        drain(correlate(c, 0))

    def terms(ti, tj, first, keep):
        rows = slice(first, first + UNIT)
        part, k = place[ti, tj]
        vis = []
        for p in (0, 1):
            if part == 0:
                value = ahead_ref[k, p, rows, :]
                vis_ref[c, part, k, p, rows, :] = value
            else:
                value = vis_ref[c, part, k, p, rows, :]
            vis.append(value.astype(jnp.float32))
        size = vis[0] * vis[0] + vis[1] * vis[1]
        size_ref[c, part, k, rows, :] = size + 1.0
        robust = 1.0 / (size + (base_ref[part, k, rows, :] - 4.0 * vis[0]))
        if keep is not None:
            robust = jnp.where(keep, robust, 0.0)
        return [robust * vis[0], robust * vis[1], robust]

    for part in range(len(parts)):
        @pl.when(c >= -part)
        def _(part=part):
            if part == 0:
                cols_ref[...] = jnp.zeros_like(cols_ref)
            if part + 1 < len(parts):
                ahead = correlate(c, part + 1)
            else:
                ahead = correlate(jnp.minimum(c + 1, last), 0)
            if part == 0:
                ahead = itertools.chain(ahead, load_channel(jnp.minimum(c + 1, last)))
            pair_sums(c, parts[part], tiles, TILE, terms, ahead, cols_ref, rows_ref)
            if part + 1 == len(parts):
                store_cols(c, cols_ref, colsum_ref)

    @pl.when(c == last)
    def _():
        totals = channel_totals(tiles, rows_ref, colsum_ref, (0.5, 0.5, 1.0))
        store_sums(totals, weight_ref[...], freq_ref[...], sums_ref)


def pieces(value):
    out = []
    for _ in range(3):
        out.append(value.astype(jnp.bfloat16).astype(jnp.float32))
        value = value - out[-1]
    return out


def next_kernel(ways, gains_ref, mask_ref, weight_ref, freq_ref, vis_ref, size_ref, *refs):
    old_refs = refs[:ways]
    (sums_ref, new_ref, fit_ref, model_ref, pair_ref, square_ref, left_ref, right_ref, cols_ref,
     rows_ref, colsum_ref) = refs[ways:]
    c = pl.program_id(0)
    last = pl.num_programs(0) - 1
    inputs = mask_ref.shape[1]
    tiles = inputs // TILE
    parts, place = tile_parts(tiles), places(tiles)
    sub = lax.broadcasted_iota(jnp.int32, (8, inputs), 0)
    zero = jnp.zeros((8, inputs), jnp.float32)

    def spread(piece, count):
        return jnp.broadcast_to(piece, (count, inputs))

    def load_channel(c):
        yield
        slot = lax.rem(c, 2)
        for p in (0, 1):
            own = model_ref[c, 8 * p : 8 * p + 8, :]
            own = jnp.concatenate([own] * 3 + [zero], axis=0).astype(jnp.bfloat16)
            for t in range(tiles):
                left_ref[slot, t, :, p * TILE : (p + 1) * TILE] = own[:, t * TILE : (t + 1) * TILE]
        right = [
            jnp.where(sub < 3, spread(model_ref[c, k : k + 1, :], 8), spread(model_ref[c, 3 + k : 4 + k, :], 8))
            for k in range(3)
        ]
        right_ref[slot] = jnp.concatenate(right + [zero], axis=0).astype(jnp.bfloat16)

    def model(c, part):
        slot = lax.rem(c, 2)
        for ti in parts[part]:
            yield
            pair = lax.dot_general(
                left_ref[slot, ti], right_ref[slot, :, ti * TILE :], (((0,), (0,)), ((), ())),
                preferred_element_type=jnp.float32,
            )
            for tj in range(ti, tiles):
                at = slice((tj - ti) * TILE, (tj - ti + 1) * TILE)
                for p in (0, 1):
                    pair_ref[place[ti, tj] + (p,)] = pair[p * TILE : (p + 1) * TILE, at]

    @pl.when(c == 0)
    def _():
        rows_ref[...] = jnp.zeros_like(rows_ref)
        old = add_up([ref[...] for ref in old_refs])
        gains = solve_update(rows_of(gains_ref, 3), [old[k : k + 1, :] for k in range(6)])
        new_ref[...] = gains
        angles = gains[1:2] + freq_ref[...] * gains[2:3]
        amplitude = gains[0:1] * mask_ref[...]
        double = amplitude + amplitude
        model_re = pieces(double * jnp.cos(angles))
        model_im = pieces(double * jnp.sin(angles))
        for k in range(3):
            model_ref[:, k, :] = model_re[k]
            model_ref[:, 3 + k, :] = model_im[k]
            model_ref[:, 8 + k, :] = model_im[k]
            model_ref[:, 11 + k, :] = -model_re[k]
        for k in (6, 7, 14, 15):
            model_ref[:, k, :] = jnp.zeros_like(angles)
        b = pieces(double * amplitude)
        b = [jnp.broadcast_to(x, (8, inputs)) for x in b]
        left = jnp.where(sub < 3, b[0], jnp.where(sub < 5, b[1], jnp.where(sub < 6, b[2], 0.0)))
        right = jnp.where(
            (sub == 0) | (sub == 3) | (sub == 5), b[0], jnp.where((sub == 1) | (sub == 4), b[1], b[2])
        )
        left = jnp.concatenate([left, zero], axis=0).astype(jnp.bfloat16)
        right = jnp.concatenate([right, zero], axis=0).astype(jnp.bfloat16)
        for ti in range(tiles):
            square = lax.dot_general(
                left[:, ti * TILE : (ti + 1) * TILE], right[:, ti * TILE :], (((0,), (0,)), ((), ())),
                preferred_element_type=jnp.float32,
            )
            for tj in range(ti, tiles):
                square_ref[place[ti, tj]] = square[:, (tj - ti) * TILE : (tj - ti + 1) * TILE]

    @pl.when(c == 0)
    def _():
        drain(load_channel(c))
        drain(model(c, 0))

    def terms(ti, tj, first, keep):
        part, k = place[ti, tj]
        rows = slice(first, first + UNIT)
        vis_re, vis_im = [vis_ref[c, part, k, p, rows, :].astype(jnp.float32) for p in (0, 1)]
        pair_re, pair_im = [pair_ref[part, k, p, rows, :] for p in (0, 1)]
        square = square_ref[part, k, rows, :]
        prod_re = vis_re * pair_re + vis_im * pair_im
        prod_im = vis_im * pair_re - vis_re * pair_im
        robust = 1.0 / (size_ref[c, part, k, rows, :] - prod_re + square)
        if keep is not None:
            robust = jnp.where(keep, robust, 0.0)
        return [robust * prod_re, robust * prod_im, robust * square]

    for part in range(len(parts)):
        @pl.when(c >= -part)
        def _(part=part):
            if part == 0:
                cols_ref[...] = jnp.zeros_like(cols_ref)
            if part + 1 < len(parts):
                ahead = model(c, part + 1)
            else:
                ahead = model(jnp.minimum(c + 1, last), 0)
            if part == 0:
                ahead = itertools.chain(ahead, load_channel(jnp.minimum(c + 1, last)))
            pair_sums(c, parts[part], tiles, 32, terms, ahead, cols_ref, rows_ref)
            if part + 1 == len(parts):
                store_cols(c, cols_ref, colsum_ref)

    @pl.when(c == last)
    def _():
        totals = channel_totals(tiles, rows_ref, colsum_ref, (0.125, 0.125, 0.25))
        store_sums(totals, weight_ref[...], freq_ref[...], sums_ref)
        bound = jnp.maximum(totals[2], 1.0)
        fit_ref[0] = totals[0] / bound
        fit_ref[1] = totals[1] / bound


def whole(shape):
    return pl.BlockSpec(shape, lambda c: (0,) * len(shape))


RESIDENT = pl.BlockSpec(memory_space=pltpu.VMEM)


def held(x):
    return pltpu.with_memory_space_constraint(x, pltpu.VMEM)


def split_kernel(volt_ref, out_ref):
    devices, _, chans, _ = out_ref.shape
    for d in range(devices):
        out_ref[d] = volt_ref[:, d * chans : (d + 1) * chans, :]


def split_channels(voltages, devices):
    inputs_dev, channels, width = voltages.shape
    chans, rows = channels // devices, max(inputs_dev // 2, 1)
    return pl.pallas_call(
        split_kernel,
        grid=(inputs_dev // rows,),
        in_specs=[pl.BlockSpec((rows, channels, width), lambda i: (i, 0, 0))],
        out_specs=pl.BlockSpec((devices, rows, chans, width), lambda i: (0, i, 0, 0)),
        out_shape=jax.ShapeDtypeStruct((devices, inputs_dev, chans, width), voltages.dtype),
        compiler_params=pltpu.CompilerParams(vmem_limit_bytes=VMEM_LIMIT),
        name="split_channels",
    )(voltages)


def first_iteration(x, mask, weight, freq):
    inputs, chans, width = x.shape
    tiles = inputs // TILE
    steps, size = len(tile_parts(tiles)), part_size(tiles)
    return pl.pallas_call(
        first_kernel,
        grid=(chans,),
        in_specs=[whole(mask.shape), whole(weight.shape), whole(freq.shape),
                  pl.BlockSpec(memory_space=pl.ANY)],
        out_specs=[RESIDENT, RESIDENT, whole((6, inputs))],
        out_shape=[
            pltpu.VMEM((chans, steps, size, 2, TILE, TILE), jnp.bfloat16),
            pltpu.VMEM((chans, steps, size, TILE, TILE), jnp.float32),
            jax.ShapeDtypeStruct((6, inputs), jnp.float32),
        ],
        scratch_shapes=[
            pltpu.VMEM((inputs, chans, width), x.dtype),
            pltpu.SemaphoreType.DMA,
            pltpu.VMEM(((inputs + 1) * chans, width), jnp.float32),
            pltpu.VMEM((2, inputs, width), jnp.bfloat16),
            pltpu.VMEM((2, tiles, 2 * TILE, width), jnp.bfloat16),
            pltpu.VMEM((inputs, TILE), jnp.float32),
            pltpu.VMEM((steps, size, TILE, TILE), jnp.float32),
            pltpu.VMEM((size, 2, TILE, TILE), jnp.bfloat16),
            pltpu.VMEM((3, 8, inputs), jnp.float32),
            pltpu.VMEM((inputs, TILE), jnp.float32),
            pltpu.VMEM((chans, 8, inputs), jnp.float32),
        ],
        compiler_params=pltpu.CompilerParams(vmem_limit_bytes=VMEM_LIMIT),
        name="first_iteration",
    )(mask, weight, freq, x)


def next_iteration(gains, old_sums, mask, weight, freq, vis, size):
    chans, steps, count = size.shape[:3]
    inputs = mask.shape[1]
    tiles = inputs // TILE
    return pl.pallas_call(
        functools.partial(next_kernel, len(old_sums)),
        grid=(chans,),
        in_specs=[whole(gains.shape), whole(mask.shape), whole(weight.shape), whole(freq.shape)]
        + [RESIDENT, RESIDENT] + [whole((6, inputs)) for _ in old_sums],
        out_specs=[whole((6, inputs)), whole((3, inputs)), whole((2, chans, inputs))],
        out_shape=[
            jax.ShapeDtypeStruct((6, inputs), jnp.float32),
            jax.ShapeDtypeStruct((3, inputs), jnp.float32),
            jax.ShapeDtypeStruct((2, chans, inputs), jnp.float32),
        ],
        scratch_shapes=[
            pltpu.VMEM((chans, 16, inputs), jnp.float32),
            pltpu.VMEM((steps, count, 2, TILE, TILE), jnp.float32),
            pltpu.VMEM((steps, count, TILE, TILE), jnp.float32),
            pltpu.VMEM((2, tiles, 32, 2 * TILE), jnp.bfloat16),
            pltpu.VMEM((2, 32, inputs), jnp.bfloat16),
            pltpu.VMEM((3, 8, inputs), jnp.float32),
            pltpu.VMEM((inputs, TILE), jnp.float32),
            pltpu.VMEM((chans, 8, inputs), jnp.float32),
        ],
        compiler_params=pltpu.CompilerParams(vmem_limit_bytes=VMEM_LIMIT),
        name="next_iteration",
    )(gains, mask, weight, freq, held(vis), held(size), *old_sums)


def add_up(parts):
    while len(parts) > 1:
        parts = [a + b for a, b in zip(parts[::2], parts[1::2])]
    return parts[0]


def all_sum(part, devices):
    if devices & (devices - 1):
        return [lax.psum(part, "chan")]
    reach = 1
    while reach < devices:
        ways = 4 if devices // reach >= 4 else 2
        got = [part] + [
            lax.ppermute(part, "chan", [(i, i ^ (k * reach)) for i in range(devices)])
            for k in range(1, ways)
        ]
        reach *= ways
        if reach == devices:
            return got
        part = add_up(got)
    return [part]


def local(voltages, antenna_usable_mask, channel_flags):
    devices = lax.axis_size("chan")
    inputs_dev, channels, sample_cols = voltages.shape
    chan_dev = channels // devices
    blocks = split_channels(voltages, devices)
    turned = lax.all_to_all(blocks, "chan", split_axis=0, concat_axis=0, tiled=True)
    inputs = inputs_dev * devices
    arrived = turned.reshape(inputs, chan_dev, sample_cols)
    first_channel = lax.axis_index("chan") * chan_dev
    channel_ids = (first_channel + jnp.arange(chan_dev)).astype(jnp.float32)
    freq = (2.0 * math.pi * (channel_ids + 0.5) / (chan_dev * devices))[:, None]
    weight = channel_flags.astype(jnp.float32)[:, None]
    mask = antenna_usable_mask.astype(jnp.float32)[None, :]
    gains = jnp.concatenate(
        [jnp.ones((1, inputs), jnp.float32), jnp.zeros((2, inputs), jnp.float32)], axis=0
    )
    vis, size, sums = first_iteration(arrived, mask, weight, freq)
    fitted = None
    for iteration in range(1, ITERS):
        sums, gains, fitted = next_iteration(
            gains, all_sum(sums, devices), mask, weight, freq, vis, size
        )
    totals = add_up(all_sum(sums, devices))
    gains = solve_rows(gains, totals)
    return (gains, fitted)


def solution(mesh):
    placed = (P(("groups", "chan"), None, None), P("groups"), P(("groups", "chan")))
    return jax.shard_map(
        local,
        mesh=mesh,
        in_specs=placed,
        out_specs=(P(None, "groups"), P(None, ("groups", "chan"), None)),
        check_vma=False,
    )
```

```python
import functools
import itertools
import math

import jax
import jax.numpy as jnp
from jax import lax
from jax.experimental import pallas as pl
from jax.experimental.pallas import tpu as pltpu
from jax.sharding import PartitionSpec as P

ITERS = 3
TILE = 128
UNIT = 16
PARTS = 2
HUGE = 1e38
VMEM_LIMIT = 16 * 1024 * 1024

huber_scale = 0.25
damping = 0.5


def solve_update(gains, sums):
    determinant = jnp.maximum(sums[3] * sums[5] - sums[4] * sums[4], 1.0)
    step_phase = (sums[5] * sums[1] - sums[4] * sums[2]) / determinant
    step_delay = (sums[3] * sums[2] - sums[4] * sums[1]) / determinant
    amplitude = gains[0] * (1.0 + damping * (sums[0] - sums[3]) / jnp.maximum(sums[3], 1.0))
    return jnp.concatenate(
        [amplitude, gains[1] + damping * step_phase, gains[2] + damping * step_delay], axis=0
    )


def solve_rows(gains, sums):
    bound = jnp.maximum(sums[3] * sums[5] - sums[4] * sums[4], 1.0)
    phase = (sums[5] * sums[1] - sums[4] * sums[2]) / bound
    delay = (sums[3] * sums[2] - sums[4] * sums[1]) / bound
    ratio = gains[0] * (sums[0] - sums[3]) / jnp.maximum(sums[3], 1.0)
    row = lax.broadcasted_iota(jnp.int32, gains.shape, 0)
    return gains + damping * jnp.where(row == 0, ratio, jnp.where(row == 1, phase, delay))


def rows_of(ref, count):
    return [ref[k : k + 1, :] for k in range(count)]


def places(tiles):
    out = {}
    for part, rows in enumerate(tile_parts(tiles)):
        pairs = [(ti, tj) for ti in rows for tj in range(ti, tiles)]
        out.update({pair: (part, k) for k, pair in enumerate(pairs)})
    return out


def part_size(tiles):
    return max(k for _, k in places(tiles).values()) + 1


def drain(jobs):
    for _ in jobs:
        pass


def pair_sums(c, rows, tiles, group, terms, ahead, cols_ref, rows_ref):
    for ti in rows:
        for first in range(0, TILE, group):
            for _ in range(1 + group // 64):
                next(ahead, None)
            row = ti * TILE + first
            totals = [None] * (group // UNIT)
            for tj in range(ti, tiles):
                parts = None
                for unit in range(group // UNIT):
                    at = first + unit * UNIT
                    keep = None
                    if tj == ti:
                        ids = lax.broadcasted_iota(jnp.int32, (UNIT, TILE), 0) + at
                        keep = ids != lax.broadcasted_iota(jnp.int32, (UNIT, TILE), 1)
                    got = terms(ti, tj, at, keep)
                    if totals[unit] is None:
                        totals[unit] = got
                    else:
                        totals[unit] = [a + b for a, b in zip(totals[unit], got)]
                    if tj > ti:
                        part = [x.reshape(UNIT // 8, 8, TILE).sum(axis=0) for x in got]
                        parts = part if parts is None else [a + b for a, b in zip(parts, part)]
                if tj > ti:
                    lanes = slice(tj * TILE, (tj + 1) * TILE)
                    for k in range(3):
                        cols_ref[k, :, lanes] += parts[k] if k != 1 else -parts[k]
            for unit in range(group // UNIT):
                fold_rows(c, row + unit * UNIT, totals[unit], rows_ref)
    drain(ahead)


def tile_parts(tiles):
    order = [r for p in range((tiles + 1) // 2) for r in sorted({p, tiles - 1 - p})]
    size = -(-len(order) // PARTS)
    return [order[k : k + size] for k in range(0, len(order), size)]


def fold_rows(c, row, totals, rows_ref):
    lanes = lax.broadcasted_iota(jnp.int32, (UNIT, TILE), 1)
    for k in range(3):
        total = jnp.broadcast_to(jnp.sum(totals[k], axis=1, keepdims=True), (UNIT, TILE))
        pltpu.store(rows_ref.at[row : row + UNIT, :], total, mask=lanes == 8 * k + c)


def store_cols(c, cols_ref, colsum_ref):
    for k in range(3):
        colsum_ref[c, k : k + 1, :] = jnp.sum(cols_ref[k], axis=0, keepdims=True)


def channel_totals(tiles, rows_ref, colsum_ref, scales):
    turned = [rows_ref[t * TILE : (t + 1) * TILE, :].T for t in range(tiles)]
    chans = colsum_ref.shape[0]
    return [
        scales[k]
        * (jnp.concatenate([t[8 * k : 8 * k + chans] for t in turned], axis=1) + colsum_ref[:, k, :])
        for k in range(3)
    ]


def store_sums(totals, weight, freq, sums_ref):
    prod_re, prod_im, curvature = totals
    wim = weight * prod_im
    wcu = weight * curvature
    sums_ref[...] = jnp.concatenate(
        [
            jnp.sum(x, axis=0, keepdims=True)
            for x in (weight * prod_re, wim, freq * wim, wcu, freq * wcu, freq * freq * wcu)
        ],
        axis=0,
    )


def first_kernel(mask_ref, weight_ref, freq_ref, arrived_ref, vis_ref, size_ref, sums_ref, x_ref, sem,
                 wide_ref, right_ref, left_ref, maskrow_ref, base_ref, ahead_ref, cols_ref,
                 rows_ref, colsum_ref):
    c = pl.program_id(0)
    inputs, chans, width = x_ref.shape
    tiles = inputs // TILE
    half = width // 2
    parts, place = tile_parts(tiles), places(tiles)
    last = chans - 1

    def load_channel(c):
        lanes = lax.broadcasted_iota(jnp.int32, (TILE, width), 1)
        slot = lax.rem(c, 2)
        for t in range(tiles):
            yield
            at = slice(t * TILE, (t + 1) * TILE)
            rows = wide_ref[pl.ds(t * TILE * chans + c, TILE, stride=chans), :]
            rows = rows * maskrow_ref[at, :]
            right_ref[slot, at, :] = rows.astype(jnp.bfloat16)
            rows = rows + rows
            turned = pltpu.roll(rows, half, 1)
            left_ref[slot, t, :TILE, :] = rows.astype(jnp.bfloat16)
            left_ref[slot, t, TILE:, :] = jnp.where(lanes < half, turned, -turned).astype(jnp.bfloat16)

    def correlate(c, part):
        slot = lax.rem(c, 2)
        for ti in parts[part]:
            yield
            twice = lax.dot_general(
                left_ref[slot, ti], right_ref[slot, ti * TILE :, :], (((1,), (1,)), ((), ())),
                preferred_element_type=jnp.float32,
            ).astype(jnp.bfloat16)
            for tj in range(ti, tiles):
                at = slice((tj - ti) * TILE, (tj - ti + 1) * TILE)
                place_part, k = place[ti, tj]
                for p in (0, 1):
                    value = twice[p * TILE : (p + 1) * TILE, at]
                    if place_part == 0:
                        ahead_ref[k, p] = value
                    else:
                        vis_ref[c, place_part, k, p] = value

    @pl.when(c == 0)
    def _():
        copy = pltpu.make_async_copy(arrived_ref, x_ref, sem)
        copy.start()
        rows_ref[...] = jnp.zeros_like(rows_ref)
        copy.wait()
        for t in range(tiles):
            at = slice(t * TILE, (t + 1) * TILE)
            block = x_ref[at].astype(jnp.float32)
            wide_ref[pl.ds(t * TILE * chans, TILE * chans), :] = block.reshape(TILE * chans, width)
            maskrow_ref[at, :] = jnp.broadcast_to(mask_ref[:, at] * 0.125, (TILE, TILE)).T
        flagged = (1.0 - mask_ref[...]) * HUGE
        ones = jnp.ones_like(flagged)
        sub = lax.broadcasted_iota(jnp.int32, (16, inputs), 0)
        near = jnp.where(sub == 0, 5.0 * ones, jnp.where(sub == 1, flagged, jnp.where(sub == 2, ones, 0.0)))
        far = jnp.where(sub < 2, ones, jnp.where(sub == 2, flagged, 0.0))
        near, far = near.astype(jnp.bfloat16), far.astype(jnp.bfloat16)
        for ti in range(tiles):
            base = lax.dot_general(
                near[:, ti * TILE : (ti + 1) * TILE], far[:, ti * TILE :], (((0,), (0,)), ((), ())),
                preferred_element_type=jnp.float32,
            )
            for tj in range(ti, tiles):
                base_ref[place[ti, tj]] = base[:, (tj - ti) * TILE : (tj - ti + 1) * TILE]

    @pl.when(c == 0)
    def _():
        drain(load_channel(c))

    @pl.when(c == 0)
    def _():
        drain(correlate(c, 0))

    def terms(ti, tj, first, keep):
        rows = slice(first, first + UNIT)
        part, k = place[ti, tj]
        vis = []
        for p in (0, 1):
            if part == 0:
                value = ahead_ref[k, p, rows, :]
                vis_ref[c, part, k, p, rows, :] = value
            else:
                value = vis_ref[c, part, k, p, rows, :]
            vis.append(value.astype(jnp.float32))
        size = vis[0] * vis[0] + vis[1] * vis[1]
        size_ref[c, part, k, rows, :] = size + 1.0
        robust = 1.0 / (size + (base_ref[part, k, rows, :] - 4.0 * vis[0]))
        if keep is not None:
            robust = jnp.where(keep, robust, 0.0)
        return [robust * vis[0], robust * vis[1], robust]

    for part in range(len(parts)):
        @pl.when(c >= -part)
        def _(part=part):
            if part == 0:
                cols_ref[...] = jnp.zeros_like(cols_ref)
            if part + 1 < len(parts):
                ahead = correlate(c, part + 1)
            else:
                ahead = correlate(jnp.minimum(c + 1, last), 0)
            if part == 0:
                ahead = itertools.chain(ahead, load_channel(jnp.minimum(c + 1, last)))
            pair_sums(c, parts[part], tiles, TILE, terms, ahead, cols_ref, rows_ref)
            if part + 1 == len(parts):
                store_cols(c, cols_ref, colsum_ref)

    @pl.when(c == last)
    def _():
        totals = channel_totals(tiles, rows_ref, colsum_ref, (0.5, 0.5, 1.0))
        store_sums(totals, weight_ref[...], freq_ref[...], sums_ref)


def pieces(value):
    out = []
    for _ in range(3):
        out.append(value.astype(jnp.bfloat16).astype(jnp.float32))
        value = value - out[-1]
    return out


def next_kernel(ways, gains_ref, mask_ref, weight_ref, freq_ref, vis_ref, size_ref, *refs):
    old_refs = refs[:ways]
    (sums_ref, new_ref, fit_ref, model_ref, pair_ref, square_ref, left_ref, right_ref, cols_ref,
     rows_ref, colsum_ref) = refs[ways:]
    c = pl.program_id(0)
    last = pl.num_programs(0) - 1
    inputs = mask_ref.shape[1]
    tiles = inputs // TILE
    parts, place = tile_parts(tiles), places(tiles)
    sub = lax.broadcasted_iota(jnp.int32, (8, inputs), 0)
    zero = jnp.zeros((8, inputs), jnp.float32)

    def spread(piece, count):
        return jnp.broadcast_to(piece, (count, inputs))

    def load_channel(c):
        yield
        slot = lax.rem(c, 2)
        for p in (0, 1):
            own = model_ref[c, 8 * p : 8 * p + 8, :]
            own = jnp.concatenate([own] * 3 + [zero], axis=0).astype(jnp.bfloat16)
            for t in range(tiles):
                left_ref[slot, t, :, p * TILE : (p + 1) * TILE] = own[:, t * TILE : (t + 1) * TILE]
        right = [
            jnp.where(sub < 3, spread(model_ref[c, k : k + 1, :], 8), spread(model_ref[c, 3 + k : 4 + k, :], 8))
            for k in range(3)
        ]
        right_ref[slot] = jnp.concatenate(right + [zero], axis=0).astype(jnp.bfloat16)

    def model(c, part):
        slot = lax.rem(c, 2)
        for ti in parts[part]:
            yield
            pair = lax.dot_general(
                left_ref[slot, ti], right_ref[slot, :, ti * TILE :], (((0,), (0,)), ((), ())),
                preferred_element_type=jnp.float32,
            )
            for tj in range(ti, tiles):
                at = slice((tj - ti) * TILE, (tj - ti + 1) * TILE)
                for p in (0, 1):
                    pair_ref[place[ti, tj] + (p,)] = pair[p * TILE : (p + 1) * TILE, at]

    @pl.when(c == 0)
    def _():
        rows_ref[...] = jnp.zeros_like(rows_ref)
        old = add_up([ref[...] for ref in old_refs])
        gains = solve_update(rows_of(gains_ref, 3), [old[k : k + 1, :] for k in range(6)])
        new_ref[...] = gains
        angles = gains[1:2] + freq_ref[...] * gains[2:3]
        amplitude = gains[0:1] * mask_ref[...]
        double = amplitude + amplitude
        model_re = pieces(double * jnp.cos(angles))
        model_im = pieces(double * jnp.sin(angles))
        for k in range(3):
            model_ref[:, k, :] = model_re[k]
            model_ref[:, 3 + k, :] = model_im[k]
            model_ref[:, 8 + k, :] = model_im[k]
            model_ref[:, 11 + k, :] = -model_re[k]
        for k in (6, 7, 14, 15):
            model_ref[:, k, :] = jnp.zeros_like(angles)
        b = pieces(double * amplitude)
        b = [jnp.broadcast_to(x, (8, inputs)) for x in b]
        left = jnp.where(sub < 3, b[0], jnp.where(sub < 5, b[1], jnp.where(sub < 6, b[2], 0.0)))
        right = jnp.where(
            (sub == 0) | (sub == 3) | (sub == 5), b[0], jnp.where((sub == 1) | (sub == 4), b[1], b[2])
        )
        left = jnp.concatenate([left, zero], axis=0).astype(jnp.bfloat16)
        right = jnp.concatenate([right, zero], axis=0).astype(jnp.bfloat16)
        for ti in range(tiles):
            square = lax.dot_general(
                left[:, ti * TILE : (ti + 1) * TILE], right[:, ti * TILE :], (((0,), (0,)), ((), ())),
                preferred_element_type=jnp.float32,
            )
            for tj in range(ti, tiles):
                square_ref[place[ti, tj]] = square[:, (tj - ti) * TILE : (tj - ti + 1) * TILE]

    @pl.when(c == 0)
    def _():
        drain(load_channel(c))
        drain(model(c, 0))

    def terms(ti, tj, first, keep):
        part, k = place[ti, tj]
        rows = slice(first, first + UNIT)
        vis_re, vis_im = [vis_ref[c, part, k, p, rows, :].astype(jnp.float32) for p in (0, 1)]
        pair_re, pair_im = [pair_ref[part, k, p, rows, :] for p in (0, 1)]
        square = square_ref[part, k, rows, :]
        prod_re = vis_re * pair_re + vis_im * pair_im
        prod_im = vis_im * pair_re - vis_re * pair_im
        robust = 1.0 / (size_ref[c, part, k, rows, :] - prod_re + square)
        if keep is not None:
            robust = jnp.where(keep, robust, 0.0)
        return [robust * prod_re, robust * prod_im, robust * square]

    for part in range(len(parts)):
        @pl.when(c >= -part)
        def _(part=part):
            if part == 0:
                cols_ref[...] = jnp.zeros_like(cols_ref)
            if part + 1 < len(parts):
                ahead = model(c, part + 1)
            else:
                ahead = model(jnp.minimum(c + 1, last), 0)
            if part == 0:
                ahead = itertools.chain(ahead, load_channel(jnp.minimum(c + 1, last)))
            pair_sums(c, parts[part], tiles, 32, terms, ahead, cols_ref, rows_ref)
            if part + 1 == len(parts):
                store_cols(c, cols_ref, colsum_ref)

    @pl.when(c == last)
    def _():
        totals = channel_totals(tiles, rows_ref, colsum_ref, (0.125, 0.125, 0.25))
        store_sums(totals, weight_ref[...], freq_ref[...], sums_ref)
        bound = jnp.maximum(totals[2], 1.0)
        fit_ref[0] = totals[0] / bound
        fit_ref[1] = totals[1] / bound


def whole(shape):
    return pl.BlockSpec(shape, lambda c: (0,) * len(shape))


RESIDENT = pl.BlockSpec(memory_space=pltpu.VMEM)


def held(x):
    return pltpu.with_memory_space_constraint(x, pltpu.VMEM)


def split_kernel(volt_ref, out_ref):
    devices, _, chans, _ = out_ref.shape
    for d in range(devices):
        out_ref[d] = volt_ref[:, d * chans : (d + 1) * chans, :]


def split_channels(voltages, devices):
    inputs_dev, channels, width = voltages.shape
    chans, rows = channels // devices, max(inputs_dev // 2, 1)
    return pl.pallas_call(
        split_kernel,
        grid=(inputs_dev // rows,),
        in_specs=[pl.BlockSpec((rows, channels, width), lambda i: (i, 0, 0))],
        out_specs=pl.BlockSpec((devices, rows, chans, width), lambda i: (0, i, 0, 0)),
        out_shape=jax.ShapeDtypeStruct((devices, inputs_dev, chans, width), voltages.dtype),
        compiler_params=pltpu.CompilerParams(vmem_limit_bytes=VMEM_LIMIT),
        name="split_channels",
    )(pltpu.with_memory_space_constraint(voltages, pltpu.HBM))


def first_iteration(x, mask, weight, freq):
    inputs, chans, width = x.shape
    tiles = inputs // TILE
    steps, size = len(tile_parts(tiles)), part_size(tiles)
    return pl.pallas_call(
        first_kernel,
        grid=(chans,),
        in_specs=[whole(mask.shape), whole(weight.shape), whole(freq.shape),
                  pl.BlockSpec(memory_space=pl.ANY)],
        out_specs=[RESIDENT, RESIDENT, whole((6, inputs))],
        out_shape=[
            pltpu.VMEM((chans, steps, size, 2, TILE, TILE), jnp.bfloat16),
            pltpu.VMEM((chans, steps, size, TILE, TILE), jnp.float32),
            jax.ShapeDtypeStruct((6, inputs), jnp.float32),
        ],
        scratch_shapes=[
            pltpu.VMEM((inputs, chans, width), x.dtype),
            pltpu.SemaphoreType.DMA,
            pltpu.VMEM(((inputs + 1) * chans, width), jnp.float32),
            pltpu.VMEM((2, inputs, width), jnp.bfloat16),
            pltpu.VMEM((2, tiles, 2 * TILE, width), jnp.bfloat16),
            pltpu.VMEM((inputs, TILE), jnp.float32),
            pltpu.VMEM((steps, size, TILE, TILE), jnp.float32),
            pltpu.VMEM((size, 2, TILE, TILE), jnp.bfloat16),
            pltpu.VMEM((3, 8, inputs), jnp.float32),
            pltpu.VMEM((inputs, TILE), jnp.float32),
            pltpu.VMEM((chans, 8, inputs), jnp.float32),
        ],
        compiler_params=pltpu.CompilerParams(vmem_limit_bytes=VMEM_LIMIT),
        name="first_iteration",
    )(mask, weight, freq, x)


def next_iteration(gains, old_sums, mask, weight, freq, vis, size):
    chans, steps, count = size.shape[:3]
    inputs = mask.shape[1]
    tiles = inputs // TILE
    return pl.pallas_call(
        functools.partial(next_kernel, len(old_sums)),
        grid=(chans,),
        in_specs=[whole(gains.shape), whole(mask.shape), whole(weight.shape), whole(freq.shape)]
        + [RESIDENT, RESIDENT] + [whole((6, inputs)) for _ in old_sums],
        out_specs=[whole((6, inputs)), whole((3, inputs)), whole((2, chans, inputs))],
        out_shape=[
            jax.ShapeDtypeStruct((6, inputs), jnp.float32),
            jax.ShapeDtypeStruct((3, inputs), jnp.float32),
            jax.ShapeDtypeStruct((2, chans, inputs), jnp.float32),
        ],
        scratch_shapes=[
            pltpu.VMEM((chans, 16, inputs), jnp.float32),
            pltpu.VMEM((steps, count, 2, TILE, TILE), jnp.float32),
            pltpu.VMEM((steps, count, TILE, TILE), jnp.float32),
            pltpu.VMEM((2, tiles, 32, 2 * TILE), jnp.bfloat16),
            pltpu.VMEM((2, 32, inputs), jnp.bfloat16),
            pltpu.VMEM((3, 8, inputs), jnp.float32),
            pltpu.VMEM((inputs, TILE), jnp.float32),
            pltpu.VMEM((chans, 8, inputs), jnp.float32),
        ],
        compiler_params=pltpu.CompilerParams(vmem_limit_bytes=VMEM_LIMIT),
        name="next_iteration",
    )(gains, mask, weight, freq, held(vis), held(size), *old_sums)


def add_up(parts):
    while len(parts) > 1:
        parts = [a + b for a, b in zip(parts[::2], parts[1::2])]
    return parts[0]


def all_sum(part, devices):
    if devices & (devices - 1):
        return [lax.psum(part, "chan")]
    reach = 1
    while reach < devices:
        ways = 4 if devices // reach >= 4 else 2
        got = [part] + [
            lax.ppermute(part, "chan", [(i, i ^ (k * reach)) for i in range(devices)])
            for k in range(1, ways)
        ]
        reach *= ways
        if reach == devices:
            return got
        part = add_up(got)
    return [part]


def local(voltages, antenna_usable_mask, channel_flags):
    devices = lax.axis_size("chan")
    inputs_dev, channels, sample_cols = voltages.shape
    chan_dev = channels // devices
    blocks = split_channels(voltages, devices)
    turned = lax.all_to_all(blocks, "chan", split_axis=0, concat_axis=0, tiled=True)
    inputs = inputs_dev * devices
    arrived = turned.reshape(inputs, chan_dev, sample_cols)
    first_channel = lax.axis_index("chan") * chan_dev
    channel_ids = (first_channel + jnp.arange(chan_dev)).astype(jnp.float32)
    freq = (2.0 * math.pi * (channel_ids + 0.5) / (chan_dev * devices))[:, None]
    weight = channel_flags.astype(jnp.float32)[:, None]
    mask = antenna_usable_mask.astype(jnp.float32)[None, :]
    gains = jnp.concatenate(
        [jnp.ones((1, inputs), jnp.float32), jnp.zeros((2, inputs), jnp.float32)], axis=0
    )
    vis, size, sums = first_iteration(arrived, mask, weight, freq)
    fitted = None
    for iteration in range(1, ITERS):
        sums, gains, fitted = next_iteration(
            gains, all_sum(sums, devices), mask, weight, freq, vis, size
        )
    totals = add_up(all_sum(sums, devices))
    gains = solve_rows(gains, totals)
    return (gains, fitted)


def solution(mesh):
    placed = (P(("groups", "chan"), None, None), P("groups"), P(("groups", "chan")))
    return jax.shard_map(
        local,
        mesh=mesh,
        in_specs=placed,
        out_specs=(P(None, "groups"), P(None, ("groups", "chan"), None)),
        check_vma=False,
    )
```
